256 devices in a mesh: grp: 4 (over y), row: 16 (over z, core), col: 4 (over x).
Axes of the slice: x: 4, y: 4, z: 8, core: 2. Of those that a mesh axis runs over, the one named last changes fastest.
Arguments:
- ocean_field: bfloat16 [256, 128, 128, 128], P('grp', 'row', 'col'), parts along dimension 0, may hold values from -6 to 6
- spec_first: bfloat16 [2, 32, 64, 64], replicated, may hold values from -0.5 to 0.5
- spec_second: bfloat16 [2, 32, 64, 64], replicated, may hold values from -0.5 to 0.5
- spec_third: bfloat16 [2, 32, 64, 64], replicated, may hold values from -0.5 to 0.5
- ffn_in: bfloat16 [64, 256], replicated, may hold values from -0.75 to 0.75
- ffn_out: bfloat16 [256, 64], replicated, may hold values from -0.375 to 0.375
- bias_in: float32 [256], replicated, may hold values from -3 to 3
- bias_out: float32 [64], replicated, may hold values from -3 to 3
Outputs:
- next_field: bfloat16 [256, 128, 128, 128], P('grp', 'row', 'col'), parts along dimension 0
The draws below stay inside these ranges and needn't reach their ends.
There are 4 independent parts, one for each index of `grp`. The reference program is written for one: setup_inputs(seed, part) draws one part's arguments, and reference() takes and returns one part's arrays. A program takes and returns all parts, laid end to end along the dimension named above; an argument that names none is the same for every part. Nothing has to cross between parts.
All inputs are finite; a program needn't handle non-finite values.
Results may differ from the reference program's by a relative error of at most 0.013.
Values may be sent and summed in bfloat16 or wider, within the bound.
A program may use at most 128 MiB of HBM per device.

```python
import math
import jax
import jax.numpy as jnp
from jax import lax

C = 64
H = 256
M = 32
N1 = 128
N2 = 128
N3 = 128


def shard_levels(rng, dims, split, least, largest):
    loudness = 1.0
    for axis_at, shards_of in split:
        steps = jax.random.uniform(jax.random.fold_in(jax.random.fold_in(rng, 6), axis_at), (shards_of,), jnp.float32, least / len(split), largest / len(split))
        loudness = loudness * jnp.repeat(jnp.exp(steps), dims[axis_at] // shards_of).reshape((-1,) + (1,) * (len(dims) - 1 - axis_at))
    return loudness


def scatter_about(key, dims, deviation, most, split=(), kind=jnp.bfloat16):
    entries = jax.random.normal(key, dims, jnp.float32) * deviation
    if len(split) > 0:
        entries = shard_levels(key, dims, split, -0.22, 0.18) * entries
    return jnp.clip(entries, min=-most, max=most).astype(kind)


def setup_inputs(seed: int = 0, part: int = 0) -> dict:
    arg_keys = jax.random.split(jax.random.key(seed), 9)
    part_splits = jax.random.split(jax.random.fold_in(arg_keys[8], part), 9)
    ocean_field = scatter_about(part_splits[0], (C, N1, N2, N3), 1.0, 6.0, ((1, 16), (2, 4)))
    spec_first = scatter_about(arg_keys[1], (2, M, C, C), (2 * C) ** -0.5, 0.5)
    spec_second = scatter_about(arg_keys[2], (2, M, C, C), (2 * C) ** -0.5, 0.5)
    spec_third = scatter_about(arg_keys[3], (2, M, C, C), (2 * C) ** -0.5, 0.5)
    ffn_in = scatter_about(arg_keys[4], (C, H), C ** -0.5, 0.75)
    ffn_out = scatter_about(arg_keys[5], (H, C), H ** -0.5, 0.375)
    bias_in = scatter_about(arg_keys[6], (H,), 0.5, 3.0, (), jnp.float32)
    bias_out = scatter_about(arg_keys[7], (C,), 0.5, 3.0, (), jnp.float32)
    return dict(ocean_field=ocean_field, spec_first=spec_first, spec_second=spec_second, spec_third=spec_third, ffn_in=ffn_in, ffn_out=ffn_out, bias_in=bias_in, bias_out=bias_out)


def forward_table(length, mode_count):
    grid_pos = jnp.arange(length, dtype=jnp.int32)[:, None]
    mode_location = jnp.arange(mode_count, dtype=jnp.int32)[None, :]
    phase = ((grid_pos * mode_location) % length).astype(jnp.float32) * (2.0 * math.pi / length)
    return jnp.stack([jnp.cos(phase), -jnp.sin(phase)], axis=1).astype(jnp.bfloat16)


def inverse_table(length, mode_count):
    mode_location = jnp.arange(mode_count, dtype=jnp.int32)[:, None]
    grid_pos = jnp.arange(length, dtype=jnp.int32)[None, :]
    phase = ((grid_pos * mode_location) % length).astype(jnp.float32) * (2.0 * math.pi / length)
    factor = jnp.where(mode_location == 0, 1.0, 2.0).astype(jnp.float32) / length
    return jnp.stack([factor * jnp.cos(phase), -factor * jnp.sin(phase)], axis=0).astype(jnp.bfloat16)


def block_weight_tensor(weight_tensor):
    real_part = weight_tensor[0]
    imag_part = weight_tensor[1]
    upper = jnp.concatenate([real_part, imag_part], axis=2)
    lower = jnp.concatenate([-imag_part, real_part], axis=2)
    return jnp.concatenate([upper, lower], axis=1)


def precise_contraction(form, left, right):
    return jnp.einsum(form, left.astype(jnp.float32), right.astype(jnp.float32), precision=lax.Precision.HIGHEST)


def along_axis(values, weight_tensor):
    channels, across, length, columns = values.shape
    mode_count = weight_tensor.shape[1]
    spectral_coefficients = precise_contraction("canq,nsm->mscaq", values, forward_table(length, mode_count))
    spectral_coefficients = spectral_coefficients.reshape(mode_count, 2 * channels, across * columns).astype(jnp.bfloat16)
    mixed_result = precise_contraction("plf,plk->pkf", spectral_coefficients, block_weight_tensor(weight_tensor))
    mixed_result = mixed_result.astype(jnp.bfloat16).reshape(mode_count, 2, channels, across, columns)
    result = precise_contraction("mscaq,smn->canq", mixed_result, inverse_table(length, mode_count))
    return result.astype(jnp.bfloat16)


def final_axis_transform(values, weight_tensor):
    channels, places, length = values.shape
    mode_count = weight_tensor.shape[1]
    spectral_coefficients = precise_contraction("cpn,nsm->mscp", values, forward_table(length, mode_count))
    spectral_coefficients = spectral_coefficients.reshape(mode_count, 2 * channels, places).astype(jnp.bfloat16)
    mixed_result = precise_contraction("plf,plk->pkf", spectral_coefficients, block_weight_tensor(weight_tensor))
    mixed_result = mixed_result.astype(jnp.bfloat16).reshape(mode_count, 2, channels, places)
    result = precise_contraction("mscp,smn->cpn", mixed_result, inverse_table(length, mode_count))
    return result.astype(jnp.bfloat16)


def feed_forward(summed, initial, ffn_in, ffn_out, bias_in, bias_out):
    def update(position, output):
        row_index = jnp.asarray(position).astype(jnp.int32)
        block = lax.dynamic_index_in_dim(summed, row_index, 1, keepdims=False)
        base = lax.dynamic_index_in_dim(initial, row_index, 1, keepdims=False)
        hidden_pre = precise_contraction("ch,ck->hk", ffn_in, block) + bias_in[:, None]
        hidden = jax.nn.gelu(hidden_pre, approximate=False).astype(jnp.bfloat16)
        result = precise_contraction("hc,hk->ck", ffn_out, hidden) + bias_out[:, None] + base.astype(jnp.float32)
        return lax.dynamic_update_index_in_dim(output, result.astype(jnp.bfloat16), row_index, 1)
    return lax.fori_loop(0, summed.shape[1], update, jnp.zeros_like(initial))


def reference(ocean_field, spec_first, spec_second, spec_third, ffn_in, ffn_out, bias_in, bias_out):
    first_part = along_axis(ocean_field.reshape(C, 1, N1, N2 * N3), spec_first).reshape(C, N1, N2, N3)
    second_part = along_axis(ocean_field, spec_second)
    third_part = final_axis_transform(ocean_field.reshape(C, N1 * N2, N3), spec_third).reshape(C, N1, N2, N3)
    pair = (first_part.astype(jnp.float32) + second_part.astype(jnp.float32)).astype(jnp.bfloat16)
    summed = (pair.astype(jnp.float32) + third_part.astype(jnp.float32)).astype(jnp.bfloat16)
    result = feed_forward(summed.reshape(C, N1, N2 * N3), ocean_field.reshape(C, N1, N2 * N3), ffn_in, ffn_out, bias_in, bias_out)
    return result.reshape(C, N1, N2, N3)
```

```python
import functools
import math

import jax
import jax.numpy as jnp
import ml_dtypes
import numpy as np
from jax import lax
from jax.experimental import pallas as pl
from jax.experimental.pallas import tpu as pltpu
from jax.sharding import PartitionSpec as P

MESH = pl.DeviceIdType.MESH
BF = jnp.bfloat16
F32 = jnp.float32
ROOT_HALF = math.sqrt(0.5)
ORDER = (8, 7, 9, 6, 10, 5, 11, 4, 12, 3, 13, 2, 14, 1, 15)


def tables(length, modes):
    n = np.arange(length, dtype=np.int32)[:, None]
    m = np.arange(modes, dtype=np.int32)[None, :]
    phase = (n * m % length).astype(np.float32) * np.float32(2.0 * math.pi / length)
    cos, sin = np.cos(phase).astype(np.float32), np.sin(phase).astype(np.float32)
    forward = np.stack([cos, -sin], axis=2).reshape(length, 2 * modes)
    factor = (np.where(m == 0, 1.0, 2.0) / length).astype(np.float32)
    inverse = np.stack([factor * cos, -factor * sin], axis=2).reshape(length, 2 * modes)
    return forward.astype(ml_dtypes.bfloat16), inverse.astype(ml_dtypes.bfloat16)


def constants(length, modes, rows, peers, half):
    forward, inverse = (t.astype(np.float32) for t in tables(length, modes))
    eye = np.eye(8, dtype=np.float32)
    k = 2 * modes
    split = forward.reshape(peers, rows, k)
    fwd_row = np.einsum("pnk,cd->kcpdn", split, eye).reshape(k * 8, length * 8)
    fwd_col = np.einsum("nk,cd->kcdn", forward, eye).reshape(k * 8, length * 8)
    split = inverse.reshape(peers, rows, k)
    inv_row = np.einsum("pnk,cd->pcnkd", split, eye).reshape(length * 8, k * 8)
    inv_col = np.einsum("nk,cd->cnkd", inverse, eye).reshape(length * 8, k * 8)
    inv_line = np.ascontiguousarray(inv_col.T)
    swap = np.zeros((half, 2, rows, 2, rows, half), np.float32)
    place = np.zeros((half, rows, rows, half), np.float32)
    for a in range(half):
        for b in range(rows):
            place[a, b, b, a] = 1.0
            for c in range(2):
                swap[a, c, b, c, b, a] = 1.0
    swap = swap.reshape(2 * half * rows, 2 * half * rows)
    place = place.reshape(half * rows, half * rows)
    return [t.astype(ml_dtypes.bfloat16) for t in (fwd_row, inv_row, fwd_col, inv_col, inv_line, swap, place)]


def dot(a, b):
    return jnp.dot(a, b, preferred_element_type=F32)


def dot_nt(a, b):
    return lax.dot_general(a, b, (((1,), (1,)), ((), ())), preferred_element_type=F32)


def dot_tn(a, b):
    return lax.dot_general(a, b, (((0,), (0,)), ((), ())), preferred_element_type=F32)


def loop(count, body, wide=1):
    def step(i, carry):
        for j in range(wide):
            body(i * wide + j)
        return carry

    lax.fori_loop(0, count // wide, step, 0)


def kernel(
    x_hbm, s1_hbm, s2_hbm, s3_hbm, ffn_in, ffn_out, bias_in, bias_out,
    fr_hbm, ir_hbm, fc_hbm, ic_hbm, il_hbm, swap, place,
    out_hbm,
    x, xs, ra, rb, back1, back2, third, spec, mix_w, fr, ir, fc, ic, il,
    widen_in, widen_out, wide_in, wide_out, hidden,
    load_sem, own_sem, out_sem, fwd_s, fwd_r, ret_s, ret_r, cf_s, cf_r, cr_s, cr_r,
):
    g, r, q = lax.axis_index("grp"), lax.axis_index("row"), lax.axis_index("col")
    loads = [
        pltpu.make_async_copy(src, dst, load_sem.at[i])
        for i, (src, dst) in enumerate(
            [
                (x_hbm, x), (s3_hbm, mix_w.at[0]), (fc_hbm, fc), (il_hbm, il), (fr_hbm, fr),
                (ir_hbm, ir), (ic_hbm, ic), (s1_hbm, mix_w.at[1]), (s2_hbm, mix_w.at[2]),
            ]
        )
    ]
    for c in loads:
        c.start()

    barrier = pltpu.get_barrier_semaphore()
    for d in range(1, 16):
        pl.semaphore_signal(barrier, inc=1, device_id=(g, lax.rem(r + d, 16), q), device_id_type=MESH)
    for d in range(1, 4):
        pl.semaphore_signal(barrier, inc=1, device_id=(g, r, lax.rem(q + d, 4)), device_id_type=MESH)

    def forward(k, t, s):
        return pltpu.make_async_remote_copy(
            xs.at[k * 16 + t], ra.at[k, s], fwd_s.at[k, t], fwd_r.at[k, s], device_id=(g, t, q), device_id_type=MESH
        )

    def give(k, t, s):
        return pltpu.make_async_remote_copy(
            ra.at[k, t], back1.at[k * 16 + s], ret_s.at[k, t], ret_r.at[k, s], device_id=(g, t, q), device_id_type=MESH
        )

    def col_forward(k, t, s):
        return pltpu.make_async_remote_copy(
            x.at[:, 2 * t + k], rb.at[k, :, s], cf_s.at[k, t], cf_r.at[k, s], device_id=(g, r, t), device_id_type=MESH
        )

    def col_give(k, t, s):
        return pltpu.make_async_remote_copy(
            rb.at[k, :, t], back2.at[:, 2 * s + k], cr_s.at[k, t], cr_r.at[k, s], device_id=(g, r, t), device_id_type=MESH
        )

    own = [pltpu.make_async_copy(xs.at[k * 16 + r], ra.at[k, r], own_sem.at[k]) for k in range(2)]
    own_back = [pltpu.make_async_copy(ra.at[k, r], back1.at[k * 16 + r], own_sem.at[2 + k]) for k in range(2)]
    own_col = [pltpu.make_async_copy(x.at[:, 2 * q + k], rb.at[k, :, q], own_sem.at[4 + k]) for k in range(2)]
    own_col_back = [
        pltpu.make_async_copy(rb.at[k, :, q], back2.at[:, 2 * q + k], own_sem.at[6 + k]) for k in range(2)
    ]

    def swapped(ref, k, i):
        parts = [
            ref[pl.ds(4 * i + 2 * j, 2), :, pl.ds(16 * k, 16), :].reshape(256, 128) for j in range(2)
        ]
        both = dot(swap[...], jnp.concatenate(parts, axis=1))
        return [both[:, 128 * j : 128 * (j + 1)].reshape(16, 16, 128) for j in range(2)]

    def to_rows(k):
        def step(i):
            for j, part in enumerate(swapped(x, k, i)):
                xs[pl.ds(16 * k, 16), pl.ds(32 * i + 16 * j, 16), :] = part.astype(BF)

        loop(16, step, 2)

    loads[0].wait()
    to_rows(0)
    pl.semaphore_wait(barrier, 18)
    for d in ORDER:
        forward(0, lax.rem(r + d, 16), r).start()
    own[0].start()
    for k in range(2):
        own_col[k].start()
        for d in range(1, 4):
            col_forward(k, lax.rem(q + d, 4), q).start()
    to_rows(1)
    for d in ORDER:
        forward(1, lax.rem(r + d, 16), r).start()
    own[1].start()

    def transposed_mix(d):
        def step(m):
            re = mix_w[d, 0, m].astype(F32)
            im = mix_w[d, 1, m].astype(F32)
            upper = jnp.concatenate([re, im], axis=1)
            lower = jnp.concatenate([-im, re], axis=1)
            return jnp.concatenate([upper, lower], axis=0).T.astype(BF)

        return step

    def mix(d):
        matrix = transposed_mix(d)

        def step(m):
            rhs = spec[pl.ds(2 * m, 2)].reshape(128, 128).astype(BF)
            spec[pl.ds(2 * m, 2)] = dot(matrix(m), rhs).reshape(2, 64, 128)

        loop(32, step, 2)

    def fold(i, result):
        spec[:, pl.ds(8 * i, 8), :] = result.reshape(64, 8, 128)

    def unfold(i):
        return spec[:, pl.ds(8 * i, 8), :].reshape(512, 128).astype(BF)

    def branch_third(k):
        def ahead(i):
            lanes = [
                x[8 * i + j, :, pl.ds(16 * k, 16), :].reshape(128, 128) for j in range(8)
            ]
            fold(i, dot_nt(fc[...], jnp.concatenate(lanes, axis=1)))

        loop(8, ahead)
        mix(0)

        def behind(i):
            turned = dot_nt(place[...], unfold(i)).astype(BF)
            result = dot(turned, il[...])
            for j in range(4):
                pair = [
                    result[:, 128 * (2 * j + e) : 128 * (2 * j + e + 1)].reshape(16, 8, 128) for e in range(2)
                ]
                third[pl.ds(16 * k, 16), pl.ds(64 * i + 16 * j, 16), :] = jnp.concatenate(pair, axis=1).astype(BF)

        loop(8, behind)

    def branch_first(k):
        def ahead(i):
            fold(i, dot(fr[...], ra[k, :, pl.ds(64 * i, 64), :].reshape(1024, 128)))

        loop(8, ahead)
        mix(1)

        def behind(i):
            ra[k, :, pl.ds(64 * i, 64), :] = dot(ir[...], unfold(i)).astype(BF).reshape(16, 64, 128)

        loop(8, behind)

    def branch_second(k):
        def ahead(i):
            fold(i, dot(fc[...], rb[k, pl.ds(8 * i, 8)].reshape(1024, 128)))

        loop(8, ahead)
        mix(2)

        def behind(i):
            rb[k, pl.ds(8 * i, 8)] = dot(ic[...], unfold(i)).astype(BF).reshape(8, 4, 32, 128)

        loop(8, behind)

    for i in (1, 2, 3):
        loads[i].wait()
    branch_third(0)
    branch_third(1)

    def spread(rows, columns):
        a = lax.broadcasted_iota(jnp.int32, (rows, columns), 0)
        b = lax.broadcasted_iota(jnp.int32, (rows, columns), 1)
        return (b // 8 == a).astype(F32).astype(BF)

    def diagonal(columns):
        a = lax.broadcasted_iota(jnp.int32, (8, columns), 0)
        b = lax.broadcasted_iota(jnp.int32, (8, columns), 1)
        return (b % 8 == a).astype(F32)

    widen_in[...] = dot_tn(ffn_in[...], spread(64, 512))
    widen_out[...] = dot_tn(ffn_out[...], spread(256, 2048))

    def widen(src, dst, columns):
        keep = diagonal(columns)

        def step(i):
            pair = [jnp.broadcast_to(src[pl.ds(2 * i + e, 1), :], (8, columns)) * keep for e in range(2)]
            dst[pl.ds(16 * i, 16), :] = jnp.concatenate(pair, axis=0).astype(BF)

        return step

    loop(128, widen(widen_in, wide_in, 512))
    loop(32, widen(widen_out, wide_out, 2048))

    for i in range(4, 9):
        loads[i].wait()

    def do_first(k):
        own[k].wait()
        for d in ORDER:
            forward(k, r, lax.rem(r + 16 - d, 16)).wait_recv()
        branch_first(k)
        for d in ORDER:
            give(k, lax.rem(r + d, 16), r).start()
        own_back[k].start()

    def do_second(k):
        own_col[k].wait()
        for d in range(1, 4):
            col_forward(k, q, lax.rem(q + d, 4)).wait_recv()
        branch_second(k)
        for d in range(1, 4):
            col_give(k, lax.rem(q + d, 4), q).start()
        own_col_back[k].start()

    do_first(0)
    do_second(0)
    do_second(1)
    do_first(1)

    for k in range(2):
        own_col_back[k].wait()
        for d in range(1, 4):
            col_give(k, q, lax.rem(q + d, 4)).wait_recv()
        for d in range(1, 4):
            col_forward(k, lax.rem(q + d, 4), q).wait_send()
        for d in ORDER:
            forward(k, lax.rem(r + d, 16), r).wait_send()

    def add_second(k):
        def step(i):
            for j, part in enumerate(swapped(back2, k, i)):
                at = (pl.ds(16 * k, 16), pl.ds(32 * i + 16 * j, 16), slice(None))
                third[at] = (third[at].astype(F32) + part).astype(BF)

        loop(16, step, 2)

    add_second(0)
    add_second(1)

    def feed(first, second):
        both = (first, second)
        lanes = [(back1[n].astype(F32) + third[n].astype(F32)).astype(BF) for n in both]
        summed = jnp.concatenate(lanes, axis=1)

        def up(i):
            at = pl.ds(256 * i, 256)
            pre = dot(wide_in[at, :], summed)
            bias = bias_in[at, :]
            pre = pre + jnp.concatenate([bias, bias], axis=1)
            hidden[at, :] = (0.5 * pre * (1.0 + lax.erf(pre * ROOT_HALF))).astype(BF)

        loop(8, up)

        def down(i):
            at = pl.ds(128 * i, 128)
            result = dot(wide_out[at, :], hidden[...])
            for j, n in enumerate(both):
                part = result[:, 128 * j : 128 * (j + 1)] + bias_out[at, :] + xs[n, at, :].astype(F32)
                xs[n, at, :] = part.astype(BF)

        loop(4, down)
        for n in both:
            pltpu.make_async_copy(xs.at[n], out_hbm.at[n], out_sem.at[n]).start()

    for k in range(2):
        own_back[k].wait()
        steps = (0,) + ORDER
        for i in range(8):
            sources = [lax.rem(r + 16 - d, 16) for d in steps[2 * i : 2 * i + 2]]
            for d, s in zip(steps[2 * i : 2 * i + 2], sources):
                if d:
                    give(k, r, s).wait_recv()
            feed(16 * k + sources[0], 16 * k + sources[1])

    for n in range(32):
        pltpu.make_async_copy(xs.at[n], out_hbm.at[n], out_sem.at[n]).wait()
    for k in range(2):
        for d in range(1, 4):
            col_give(k, lax.rem(q + d, 4), q).wait_send()
        for d in ORDER:
            give(k, lax.rem(r + d, 16), r).wait_send()


def body(ocean_field, spec_first, spec_second, spec_third, ffn_in, ffn_out, bias_in, bias_out):
    consts = constants(128, 32, 8, 16, 16)
    wide_bias_in = jnp.broadcast_to(jnp.repeat(bias_in, 8)[:, None], (2048, 128))
    wide_bias_out = jnp.broadcast_to(jnp.repeat(bias_out, 8)[:, None], (512, 128))
    anywhere, vmem = pl.BlockSpec(memory_space=pl.ANY), pl.BlockSpec(memory_space=pltpu.VMEM)
    dma = pltpu.SemaphoreType.DMA
    scratch = [
        pltpu.VMEM((64, 8, 32, 128), BF),
        pltpu.VMEM((32, 512, 128), BF),
        pltpu.VMEM((2, 16, 512, 128), BF),
        pltpu.VMEM((2, 64, 4, 32, 128), BF),
        pltpu.VMEM((32, 512, 128), BF),
        pltpu.VMEM((64, 8, 32, 128), BF),
        pltpu.VMEM((32, 512, 128), BF),
        pltpu.VMEM((64, 64, 128), F32),
        pltpu.VMEM((3, 2, 32, 64, 64), BF),
        pltpu.VMEM((512, 1024), BF),
        pltpu.VMEM((1024, 512), BF),
        pltpu.VMEM((512, 1024), BF),
        pltpu.VMEM((1024, 512), BF),
        pltpu.VMEM((512, 1024), BF),
        pltpu.VMEM((256, 512), F32),
        pltpu.VMEM((64, 2048), F32),
        pltpu.VMEM((2048, 512), BF),
        pltpu.VMEM((512, 2048), BF),
        pltpu.VMEM((2048, 256), BF),
        dma((9,)), dma((8,)), dma((32,)),
        dma((2, 16)), dma((2, 16)), dma((2, 16)), dma((2, 16)),
        dma((2, 4)), dma((2, 4)), dma((2, 4)), dma((2, 4)),
    ]
    result = pl.pallas_call(
        kernel,
        out_shape=jax.ShapeDtypeStruct((32, 512, 128), BF),
        in_specs=[anywhere] * 4 + [vmem] * 4 + [anywhere] * 5 + [vmem] * 2,
        out_specs=anywhere,
        scratch_shapes=scratch,
        compiler_params=pltpu.CompilerParams(
            collective_id=0, has_side_effects=True, vmem_limit_bytes=60 * 2**20
        ),
        name="fno_layer",
    )(
        ocean_field, spec_first, spec_second, spec_third, ffn_in, ffn_out, wide_bias_in, wide_bias_out,
        *[jnp.asarray(c) for c in consts],
    )
    return result.reshape(32, 64, 8, 128).transpose(1, 2, 0, 3)


def solution(mesh):
    return jax.shard_map(
        body,
        mesh=mesh,
        in_specs=(P("grp", "row", "col", None), P(), P(), P(), P(), P(), P(), P()),
        out_specs=P("grp", "row", "col", None),
        check_vma=False,
    )
```

```python
import functools
import math

import jax
import jax.numpy as jnp
import ml_dtypes
import numpy as np
from jax import lax
from jax.experimental import pallas as pl
from jax.experimental.pallas import tpu as pltpu
from jax.sharding import PartitionSpec as P

MESH = pl.DeviceIdType.MESH
BF = jnp.bfloat16
F32 = jnp.float32
ROOT_HALF = math.sqrt(0.5)
ORDER = (8, 7, 9, 6, 10, 5, 11, 4, 12, 3, 13, 2, 14, 1, 15)


def tables(length, modes):
    n = np.arange(length, dtype=np.int32)[:, None]
    m = np.arange(modes, dtype=np.int32)[None, :]
    phase = (n * m % length).astype(np.float32) * np.float32(2.0 * math.pi / length)
    cos, sin = np.cos(phase).astype(np.float32), np.sin(phase).astype(np.float32)
    forward = np.stack([cos, -sin], axis=2).reshape(length, 2 * modes)
    factor = (np.where(m == 0, 1.0, 2.0) / length).astype(np.float32)
    inverse = np.stack([factor * cos, -factor * sin], axis=2).reshape(length, 2 * modes)
    return forward.astype(ml_dtypes.bfloat16), inverse.astype(ml_dtypes.bfloat16)


def constants(length, modes, rows, peers, half):
    forward, inverse = (t.astype(np.float32) for t in tables(length, modes))
    eye = np.eye(8, dtype=np.float32)
    k = 2 * modes
    split = forward.reshape(peers, rows, k)
    fwd_row = np.einsum("pnk,cd->kcpdn", split, eye).reshape(k * 8, length * 8)
    fwd_col = np.einsum("nk,cd->kcdn", forward, eye).reshape(k * 8, length * 8)
    split = inverse.reshape(peers, rows, k)
    inv_row = np.einsum("pnk,cd->pcnkd", split, eye).reshape(length * 8, k * 8)
    inv_col = np.einsum("nk,cd->cnkd", inverse, eye).reshape(length * 8, k * 8)
    inv_line = np.ascontiguousarray(inv_col.T)
    swap = np.zeros((half, 2, rows, 2, rows, half), np.float32)
    place = np.zeros((half, rows, rows, half), np.float32)
    for a in range(half):
        for b in range(rows):
            place[a, b, b, a] = 1.0
            for c in range(2):
                swap[a, c, b, c, b, a] = 1.0
    swap = swap.reshape(2 * half * rows, 2 * half * rows)
    place = place.reshape(half * rows, half * rows)
    return [t.astype(ml_dtypes.bfloat16) for t in (fwd_row, inv_row, fwd_col, inv_col, inv_line, swap, swap.T, place)]


def dot(a, b):
    return jnp.dot(a, b, preferred_element_type=F32)


def dot_nt(a, b):
    return lax.dot_general(a, b, (((1,), (1,)), ((), ())), preferred_element_type=F32)


def dot_tn(a, b):
    return lax.dot_general(a, b, (((0,), (0,)), ((), ())), preferred_element_type=F32)


def loop(count, body, wide=1):
    def step(i, carry):
        for j in range(wide):
            body(i * wide + j)
        return carry

    lax.fori_loop(0, count // wide, step, 0)


def kernel(
    x_hbm, s1_hbm, s2_hbm, s3_hbm, fi_hbm, fo_hbm, bi_hbm, bo_hbm,
    swap_hbm, back_hbm, place_hbm, fr_hbm, ir_hbm, fc_hbm, ic_hbm, il_hbm,
    out_hbm,
    x, xs, ra, rb, back1, back2, third, spec, mix_w, swap, swap_back, place, fr, ir, fc, ic, il,
    ffn_in, ffn_out, row_in, row_out, bias_in, bias_out,
    widen_in, widen_out, wide_in, wide_out, hidden,
    load_sem, own_sem, out_sem, fwd_s, fwd_r, ret_s, ret_r, cf_s, cf_r, cr_s, cr_r,
):
    g, r, q = lax.axis_index("grp"), lax.axis_index("row"), lax.axis_index("col")
    loads = [
        pltpu.make_async_copy(src, dst, load_sem.at[i])
        for i, (src, dst) in enumerate(
            [
                (x_hbm, x), (swap_hbm, swap), (s3_hbm, mix_w.at[0]), (fc_hbm, fc), (il_hbm, il), (place_hbm, place),
                (fi_hbm, ffn_in), (fo_hbm, ffn_out), (bi_hbm, row_in), (bo_hbm, row_out), (fr_hbm, fr),
                (ir_hbm, ir), (ic_hbm, ic), (s1_hbm, mix_w.at[1]), (s2_hbm, mix_w.at[2]), (back_hbm, swap_back),
            ]
        )
    ]
    for c in loads:
        c.start()

    barrier = pltpu.get_barrier_semaphore()
    for d in range(1, 16):
        pl.semaphore_signal(barrier, inc=1, device_id=(g, lax.rem(r + d, 16), q), device_id_type=MESH)
    for d in range(1, 4):
        pl.semaphore_signal(barrier, inc=1, device_id=(g, r, lax.rem(q + d, 4)), device_id_type=MESH)

    def forward(k, t, s):
        return pltpu.make_async_remote_copy(
            xs.at[k * 16 + t], ra.at[k, s], fwd_s.at[k, t], fwd_r.at[k, s], device_id=(g, t, q), device_id_type=MESH
        )

    def give(k, t, s):
        return pltpu.make_async_remote_copy(
            ra.at[k, t], back1.at[k * 16 + s], ret_s.at[k, t], ret_r.at[k, s], device_id=(g, t, q), device_id_type=MESH
        )

    def col_forward(k, t, s):
        return pltpu.make_async_remote_copy(
            x.at[:, 2 * t + k], rb.at[k, :, s], cf_s.at[k, t], cf_r.at[k, s], device_id=(g, r, t), device_id_type=MESH
        )

    def col_give(k, t, s):
        return pltpu.make_async_remote_copy(
            rb.at[k, :, t], back2.at[:, 2 * s + k], cr_s.at[k, t], cr_r.at[k, s], device_id=(g, r, t), device_id_type=MESH
        )

    own = [pltpu.make_async_copy(xs.at[k * 16 + r], ra.at[k, r], own_sem.at[k]) for k in range(2)]
    own_back = [pltpu.make_async_copy(ra.at[k, r], back1.at[k * 16 + r], own_sem.at[2 + k]) for k in range(2)]
    own_col = [pltpu.make_async_copy(x.at[:, 2 * q + k], rb.at[k, :, q], own_sem.at[4 + k]) for k in range(2)]
    own_col_back = [
        pltpu.make_async_copy(rb.at[k, :, q], back2.at[:, 2 * q + k], own_sem.at[6 + k]) for k in range(2)
    ]

    def swapped(ref, k, i):
        parts = [
            ref[pl.ds(4 * i + 2 * j, 2), :, pl.ds(16 * k, 16), :].reshape(256, 128) for j in range(2)
        ]
        both = dot(swap[...], jnp.concatenate(parts, axis=1))
        return [both[:, 128 * j : 128 * (j + 1)].reshape(16, 16, 128) for j in range(2)]

    def to_rows(k):
        def step(i):
            for j, part in enumerate(swapped(x, k, i)):
                xs[pl.ds(16 * k, 16), pl.ds(32 * i + 16 * j, 16), :] = part.astype(BF)

        loop(16, step, 2)

    loads[0].wait()
    loads[1].wait()
    to_rows(0)
    pl.semaphore_wait(barrier, 18)
    for d in ORDER:
        forward(0, lax.rem(r + d, 16), r).start()
    own[0].start()
    for k in range(2):
        own_col[k].start()
        for d in range(1, 4):
            col_forward(k, lax.rem(q + d, 4), q).start()
    to_rows(1)
    for d in ORDER:
        forward(1, lax.rem(r + d, 16), r).start()
    own[1].start()

    def transposed_mix(d):
        def step(m):
            re = mix_w[d, 0, m].astype(F32)
            im = mix_w[d, 1, m].astype(F32)
            upper = jnp.concatenate([re, im], axis=1)
            lower = jnp.concatenate([-im, re], axis=1)
            return jnp.concatenate([upper, lower], axis=0).T.astype(BF)

        return step

    def mix(d):
        matrix = transposed_mix(d)

        def step(m):
            rhs = spec[pl.ds(2 * m, 2)].reshape(128, 128).astype(BF)
            spec[pl.ds(2 * m, 2)] = dot(matrix(m), rhs).reshape(2, 64, 128)

        loop(32, step, 2)

    def fold(i, result):
        spec[:, pl.ds(8 * i, 8), :] = result.reshape(64, 8, 128)

    def unfold(i):
        return spec[:, pl.ds(8 * i, 8), :].reshape(512, 128).astype(BF)

    def branch_third(k):
        def ahead(i):
            lanes = [
                x[8 * i + j, :, pl.ds(16 * k, 16), :].reshape(128, 128) for j in range(8)
            ]
            fold(i, dot_nt(fc[...], jnp.concatenate(lanes, axis=1)))

        loop(8, ahead)
        mix(0)

        def behind(i):
            turned = dot_nt(place[...], unfold(i)).astype(BF)
            result = dot(turned, il[...])
            for j in range(4):
                pair = [
                    result[:, 128 * (2 * j + e) : 128 * (2 * j + e + 1)].reshape(16, 8, 128) for e in range(2)
                ]
                third[pl.ds(16 * k, 16), pl.ds(64 * i + 16 * j, 16), :] = jnp.concatenate(pair, axis=1).astype(BF)

        loop(8, behind)

    def branch_first(k):
        def ahead(i):
            fold(i, dot(fr[...], ra[k, :, pl.ds(64 * i, 64), :].reshape(1024, 128)))

        loop(8, ahead)
        mix(1)

        def behind(i):
            ra[k, :, pl.ds(64 * i, 64), :] = dot(ir[...], unfold(i)).astype(BF).reshape(16, 64, 128)

        loop(8, behind)

    def branch_second(k):
        def ahead(i):
            fold(i, dot(fc[...], rb[k, pl.ds(8 * i, 8)].reshape(1024, 128)))

        loop(8, ahead)
        mix(2)

        def behind(i):
            rb[k, pl.ds(8 * i, 8)] = dot(ic[...], unfold(i)).astype(BF).reshape(8, 4, 32, 128)

        loop(8, behind)

    for i in range(2, 10):
        loads[i].wait()
    branch_third(0)
    branch_third(1)

    def spread(rows, columns):
        a = lax.broadcasted_iota(jnp.int32, (rows, columns), 0)
        b = lax.broadcasted_iota(jnp.int32, (rows, columns), 1)
        return (b // 8 == a).astype(F32).astype(BF)

    def diagonal(columns):
        a = lax.broadcasted_iota(jnp.int32, (8, columns), 0)
        b = lax.broadcasted_iota(jnp.int32, (8, columns), 1)
        return (b % 8 == a).astype(F32)

    widen_in[...] = dot_tn(ffn_in[...], spread(64, 512))
    widen_out[...] = dot(ffn_out[...], spread(256, 2048))

    def widen(src, dst, columns):
        keep = diagonal(columns)

        def step(i):
            pair = [jnp.broadcast_to(src[pl.ds(2 * i + e, 1), :], (8, columns)) * keep for e in range(2)]
            dst[pl.ds(16 * i, 16), :] = jnp.concatenate(pair, axis=0).astype(BF)

        return step

    loop(128, widen(widen_in, wide_in, 512))
    loop(32, widen(widen_out, wide_out, 2048))

    def spread_bias(src, dst, count):
        def step(i):
            rows = lax.broadcasted_iota(jnp.int32, (256, count), 0) + 256 * i
            picked = lax.broadcasted_iota(jnp.int32, (256, count), 1) == rows // 8
            values = jnp.where(picked, jnp.broadcast_to(src[...], (256, count)), 0.0)
            dst[pl.ds(256 * i, 256), :] = jnp.broadcast_to(jnp.sum(values, axis=1, keepdims=True), (256, 128))

        loop(8 * count // 256, step)

    spread_bias(row_in, bias_in, 256)
    spread_bias(row_out, bias_out, 64)

    for i in range(10, 16):
        loads[i].wait()

    def do_first(k):
        own[k].wait()
        for d in ORDER:
            forward(k, r, lax.rem(r + 16 - d, 16)).wait_recv()
        branch_first(k)
        for d in ORDER:
            give(k, lax.rem(r + d, 16), r).start()
        own_back[k].start()

    def do_second(k):
        own_col[k].wait()
        for d in range(1, 4):
            col_forward(k, q, lax.rem(q + d, 4)).wait_recv()
        branch_second(k)
        for d in range(1, 4):
            col_give(k, lax.rem(q + d, 4), q).start()
        own_col_back[k].start()

    do_first(0)
    do_second(0)
    do_second(1)
    do_first(1)

    for k in range(2):
        own_col_back[k].wait()
        for d in range(1, 4):
            col_give(k, q, lax.rem(q + d, 4)).wait_recv()
        for d in range(1, 4):
            col_forward(k, lax.rem(q + d, 4), q).wait_send()
        for d in ORDER:
            forward(k, lax.rem(r + d, 16), r).wait_send()

    def add_second(k):
        def step(i):
            for j, part in enumerate(swapped(back2, k, i)):
                at = (pl.ds(16 * k, 16), pl.ds(32 * i + 16 * j, 16), slice(None))
                third[at] = (third[at].astype(F32) + part).astype(BF)

        loop(16, step, 2)

    add_second(0)
    add_second(1)

    def feed(first, second):
        both = (first, second)
        lanes = [(back1[n].astype(F32) + third[n].astype(F32)).astype(BF) for n in both]
        summed = jnp.concatenate(lanes, axis=1)

        def up(i):
            at = pl.ds(512 * i, 512)
            pre = dot(wide_in[at, :], summed)
            bias = bias_in[at, :]
            pre = pre + jnp.concatenate([bias, bias], axis=1)
            hidden[at, :] = (0.5 * pre * (1.0 + lax.erf(pre * ROOT_HALF))).astype(BF)

        loop(4, up)

        result = dot(wide_out[...], hidden[...])
        for j, n in enumerate(both):
            part = result[:, 128 * j : 128 * (j + 1)] + bias_out[...] + xs[n].astype(F32)
            xs[n] = part.astype(BF)

    def out_copy(k, i):
        at = (pl.ds(4 * i, 4), slice(None), pl.ds(16 * k, 16), slice(None))
        return pltpu.make_async_copy(x.at[at], out_hbm.at[at], out_sem.at[k, i])

    def to_cells(k):
        def step(i):
            parts = [xs[pl.ds(16 * k, 16), pl.ds(32 * i + 16 * j, 16), :].reshape(256, 128) for j in range(2)]
            both = dot(swap_back[...], jnp.concatenate(parts, axis=1))
            for j in range(2):
                cells = both[:, 128 * j : 128 * (j + 1)].astype(BF).reshape(2, 8, 16, 128)
                x[pl.ds(4 * i + 2 * j, 2), :, pl.ds(16 * k, 16), :] = cells
            out_copy(k, i).start()

        loop(16, step, 2)

    for k in range(2):
        own_back[k].wait()
        steps = (0,) + ORDER
        for i in range(8):
            sources = [lax.rem(r + 16 - d, 16) for d in steps[2 * i : 2 * i + 2]]
            for d, s in zip(steps[2 * i : 2 * i + 2], sources):
                if d:
                    give(k, r, s).wait_recv()
            feed(16 * k + sources[0], 16 * k + sources[1])
        to_cells(k)

    for k in range(2):
        loop(16, lambda i: out_copy(k, i).wait())
    for k in range(2):
        for d in range(1, 4):
            col_give(k, lax.rem(q + d, 4), q).wait_send()
        for d in ORDER:
            give(k, lax.rem(r + d, 16), r).wait_send()


def body(ocean_field, spec_first, spec_second, spec_third, ffn_in, ffn_out, bias_in, bias_out):
    consts = constants(128, 32, 8, 16, 16)
    fwd_row, inv_row, fwd_col, inv_col, inv_line, swap, swap_back, place = (jnp.asarray(c) for c in consts)
    anywhere = pl.BlockSpec(memory_space=pl.ANY)
    dma = pltpu.SemaphoreType.DMA
    scratch = [
        pltpu.VMEM((64, 8, 32, 128), BF),
        pltpu.VMEM((32, 512, 128), BF),
        pltpu.VMEM((2, 16, 512, 128), BF),
        pltpu.VMEM((2, 64, 4, 32, 128), BF),
        pltpu.VMEM((32, 512, 128), BF),
        pltpu.VMEM((64, 8, 32, 128), BF),
        pltpu.VMEM((32, 512, 128), BF),
        pltpu.VMEM((64, 64, 128), F32),
        pltpu.VMEM((3, 2, 32, 64, 64), BF),
        pltpu.VMEM((256, 256), BF),
        pltpu.VMEM((256, 256), BF),
        pltpu.VMEM((128, 128), BF),
        pltpu.VMEM((512, 1024), BF),
        pltpu.VMEM((1024, 512), BF),
        pltpu.VMEM((512, 1024), BF),
        pltpu.VMEM((1024, 512), BF),
        pltpu.VMEM((512, 1024), BF),
        pltpu.VMEM((64, 256), BF),
        pltpu.VMEM((64, 256), BF),
        pltpu.VMEM((1, 256), F32),
        pltpu.VMEM((1, 64), F32),
        pltpu.VMEM((2048, 128), F32),
        pltpu.VMEM((512, 128), F32),
        pltpu.VMEM((256, 512), F32),
        pltpu.VMEM((64, 2048), F32),
        pltpu.VMEM((2048, 512), BF),
        pltpu.VMEM((512, 2048), BF),
        pltpu.VMEM((2048, 256), BF),
        dma((16,)), dma((8,)), dma((2, 16)),
        dma((2, 16)), dma((2, 16)), dma((2, 16)), dma((2, 16)),
        dma((2, 4)), dma((2, 4)), dma((2, 4)), dma((2, 4)),
    ]
    return pl.pallas_call(
        kernel,
        out_shape=jax.ShapeDtypeStruct(ocean_field.shape, BF),
        in_specs=[anywhere] * 16,
        out_specs=anywhere,
        scratch_shapes=scratch,
        compiler_params=pltpu.CompilerParams(
            collective_id=0, has_side_effects=True, vmem_limit_bytes=60 * 2**20
        ),
        name="fno_layer",
    )(
        ocean_field, spec_first, spec_second, spec_third, ffn_in, ffn_out.T, bias_in[None, :], bias_out[None, :],
        swap, swap_back, place, fwd_row, inv_row, fwd_col, inv_col, inv_line,
    )


def solution(mesh):
    return jax.shard_map(
        body,
        mesh=mesh,
        in_specs=(P("grp", "row", "col", None), P(), P(), P(), P(), P(), P(), P()),
        out_specs=P("grp", "row", "col", None),
        check_vma=False,
    )
```

```python
import functools
import math

import jax
import jax.numpy as jnp
import ml_dtypes
import numpy as np
from jax import lax
from jax.experimental import pallas as pl
from jax.experimental.pallas import tpu as pltpu
from jax.sharding import PartitionSpec as P

MESH = pl.DeviceIdType.MESH
BF = jnp.bfloat16
F32 = jnp.float32
ROOT_HALF = math.sqrt(0.5)
ORDER = (8, 7, 9, 6, 10, 5, 11, 4, 12, 3, 13, 2, 14, 1, 15)


def tables(length, modes):
    n = np.arange(length, dtype=np.int32)[:, None]
    m = np.arange(modes, dtype=np.int32)[None, :]
    phase = (n * m % length).astype(np.float32) * np.float32(2.0 * math.pi / length)
    cos, sin = np.cos(phase).astype(np.float32), np.sin(phase).astype(np.float32)
    forward = np.stack([cos, -sin], axis=2).reshape(length, 2 * modes)
    factor = (np.where(m == 0, 1.0, 2.0) / length).astype(np.float32)
    inverse = np.stack([factor * cos, -factor * sin], axis=2).reshape(length, 2 * modes)
    return forward.astype(ml_dtypes.bfloat16), inverse.astype(ml_dtypes.bfloat16)


def constants(length, modes, rows, peers, half):
    forward, inverse = (t.astype(np.float32) for t in tables(length, modes))
    eye = np.eye(8, dtype=np.float32)
    k = 2 * modes
    split = forward.reshape(peers, rows, k)
    fwd_row = np.einsum("pnk,cd->kcpdn", split, eye).reshape(k * 8, length * 8)
    fwd_col = np.einsum("nk,cd->kcdn", forward, eye).reshape(k * 8, length * 8)
    split = inverse.reshape(peers, rows, k)
    inv_row = np.einsum("pnk,cd->pcnkd", split, eye).reshape(length * 8, k * 8)
    inv_col = np.einsum("nk,cd->cnkd", inverse, eye).reshape(length * 8, k * 8)
    inv_line = np.ascontiguousarray(inv_col.T)
    swap = np.zeros((half, 2, rows, 2, rows, half), np.float32)
    place = np.zeros((half, rows, rows, half), np.float32)
    for a in range(half):
        for b in range(rows):
            place[a, b, b, a] = 1.0
            for c in range(2):
                swap[a, c, b, c, b, a] = 1.0
    swap = swap.reshape(2 * half * rows, 2 * half * rows)
    place = place.reshape(half * rows, half * rows)
    return [t.astype(ml_dtypes.bfloat16) for t in (fwd_row, inv_row, fwd_col, inv_col, inv_line, swap, swap.T, place)]


def dot(a, b):
    return jnp.dot(a, b, preferred_element_type=F32)


def dot_nt(a, b):
    return lax.dot_general(a, b, (((1,), (1,)), ((), ())), preferred_element_type=F32)


def dot_tn(a, b):
    return lax.dot_general(a, b, (((0,), (0,)), ((), ())), preferred_element_type=F32)


def loop(count, body, wide=1):
    def step(i, carry):
        for j in range(wide):
            body(i * wide + j)
        return carry

    lax.fori_loop(0, count // wide, step, 0)


def restored(swap_back, blocks):
    both = dot(swap_back[...], jnp.concatenate([b.reshape(256, 128) for b in blocks], axis=1))
    return [both[:, 128 * j : 128 * (j + 1)].astype(BF).reshape(2, 8, 16, 128) for j in range(2)]


def finish(back_hbm, cells, rows, out, swap_back, held, staged, table_sem, cell_sem, load_sem, out_sem):
    table = pltpu.make_async_copy(back_hbm, swap_back, table_sem)

    def load(i):
        at = (slice(None), pl.ds(64 * i, 64))
        return pltpu.make_async_copy(rows.at[at], held.at[at], load_sem.at[i])

    def move(i):
        at = pl.ds(8 * i, 8)
        return pltpu.make_async_copy(cells.at[at], staged.at[at, :, 0:16], cell_sem.at[i])

    def store(i):
        at = pl.ds(8 * i, 8)
        return pltpu.make_async_copy(staged.at[at], out.at[at], out_sem.at[i])

    table.start()
    for i in range(8):
        load(i).start()
        move(i).start()
    table.wait()

    def step(i):
        load(i).wait()
        for e in range(2):
            blocks = [held[:, pl.ds(64 * i + 32 * e + 16 * j, 16), :] for j in range(2)]
            for j, part in enumerate(restored(swap_back, blocks)):
                staged[pl.ds(8 * i + 4 * e + 2 * j, 2), :, 16:32, :] = part
        move(i).wait()
        store(i).start()

    loop(8, step, 2)
    for i in range(8):
        store(i).wait()


def kernel(
    x_hbm, s1_hbm, s2_hbm, s3_hbm, fi_hbm, fo_hbm, bi_hbm, bo_hbm,
    swap_hbm, back_hbm, place_hbm, fr_hbm, ir_hbm, fc_hbm, ic_hbm, il_hbm,
    out_cells, out_rows,
    x, xs, ra, rb, back1, back2, third, spec, mix_w, swap, swap_back, place, fr, ir, fc, ic, il,
    ffn_in, ffn_out, row_in, row_out, bias_in, bias_out,
    widen_in, widen_out, wide_in, wide_out, hidden,
    load_sem, own_sem, out_sem, fwd_s, fwd_r, ret_s, ret_r, cf_s, cf_r, cr_s, cr_r,
):
    g, r, q = lax.axis_index("grp"), lax.axis_index("row"), lax.axis_index("col")
    loads = [
        pltpu.make_async_copy(src, dst, load_sem.at[i])
        for i, (src, dst) in enumerate(
            [
                (x_hbm.at[:32], x.at[:32]), (swap_hbm, swap), (x_hbm.at[32:], x.at[32:]), (s3_hbm, mix_w.at[0]), (fc_hbm, fc), (il_hbm, il), (place_hbm, place),
                (fi_hbm, ffn_in), (fo_hbm, ffn_out), (bi_hbm, row_in), (bo_hbm, row_out), (fr_hbm, fr),
                (ir_hbm, ir), (ic_hbm, ic), (s1_hbm, mix_w.at[1]), (s2_hbm, mix_w.at[2]), (back_hbm, swap_back),
            ]
        )
    ]
    for c in loads:
        c.start()

    barrier = pltpu.get_barrier_semaphore()
    for d in range(1, 16):
        pl.semaphore_signal(barrier, inc=1, device_id=(g, lax.rem(r + d, 16), q), device_id_type=MESH)
    for d in range(1, 4):
        pl.semaphore_signal(barrier, inc=1, device_id=(g, r, lax.rem(q + d, 4)), device_id_type=MESH)

    def forward(part, t, s):
        k, at = ((0, pl.ds(0, 256)), (0, pl.ds(256, 256)), (1, pl.ds(0, 512)))[part]
        return pltpu.make_async_remote_copy(
            xs.at[k * 16 + t, at], ra.at[k, s, at], fwd_s.at[part, t], fwd_r.at[part, s],
            device_id=(g, t, q), device_id_type=MESH,
        )

    parts_of = ((0, 1), (2,))

    def give(k, t, s):
        return pltpu.make_async_remote_copy(
            ra.at[k, t], back1.at[k * 16 + s], ret_s.at[k, t], ret_r.at[k, s], device_id=(g, t, q), device_id_type=MESH
        )

    def col_forward(k, t, s):
        return pltpu.make_async_remote_copy(
            x.at[:, 2 * t + k], rb.at[k, :, s], cf_s.at[k, t], cf_r.at[k, s], device_id=(g, r, t), device_id_type=MESH
        )

    def col_give(k, t, s):
        return pltpu.make_async_remote_copy(
            rb.at[k, :, t], back2.at[:, 2 * s + k], cr_s.at[k, t], cr_r.at[k, s], device_id=(g, r, t), device_id_type=MESH
        )

    own = [pltpu.make_async_copy(xs.at[k * 16 + r], ra.at[k, r], own_sem.at[k]) for k in range(2)]
    own_back = [pltpu.make_async_copy(ra.at[k, r], back1.at[k * 16 + r], own_sem.at[2 + k]) for k in range(2)]
    own_col = [pltpu.make_async_copy(x.at[:, 2 * q + k], rb.at[k, :, q], own_sem.at[4 + k]) for k in range(2)]
    own_col_back = [
        pltpu.make_async_copy(rb.at[k, :, q], back2.at[:, 2 * q + k], own_sem.at[6 + k]) for k in range(2)
    ]

    def swapped(ref, k, i):
        parts = [
            ref[pl.ds(4 * i + 2 * j, 2), :, pl.ds(16 * k, 16), :].reshape(256, 128) for j in range(2)
        ]
        both = dot(swap[...], jnp.concatenate(parts, axis=1))
        return [both[:, 128 * j : 128 * (j + 1)].reshape(16, 16, 128) for j in range(2)]

    def to_rows(k, start, count):
        def step(i):
            for j, part in enumerate(swapped(x, k, start + i)):
                xs[pl.ds(16 * k, 16), pl.ds(32 * (start + i) + 16 * j, 16), :] = part.astype(BF)

        loop(count, step, 4)

    loads[0].wait()
    loads[1].wait()
    to_rows(0, 0, 8)
    pl.semaphore_wait(barrier, 18)
    for d in ORDER:
        forward(0, lax.rem(r + d, 16), r).start()
    loads[2].wait()
    to_rows(0, 8, 8)
    for d in ORDER:
        forward(1, lax.rem(r + d, 16), r).start()
    own[0].start()
    for k in range(2):
        own_col[k].start()
        for d in range(1, 4):
            col_forward(k, lax.rem(q + d, 4), q).start()
    to_rows(1, 0, 16)
    for d in ORDER:
        forward(2, lax.rem(r + d, 16), r).start()
    own[1].start()

    def transposed_mix(d):
        def step(m):
            re = mix_w[d, 0, m].astype(F32)
            im = mix_w[d, 1, m].astype(F32)
            upper = jnp.concatenate([re, im], axis=1)
            lower = jnp.concatenate([-im, re], axis=1)
            return jnp.concatenate([upper, lower], axis=0).T.astype(BF)

        return step

    def mix(d):
        matrix = transposed_mix(d)

        def step(m):
            rhs = spec[pl.ds(2 * m, 2)].reshape(128, 128).astype(BF)
            spec[pl.ds(2 * m, 2)] = dot(matrix(m), rhs).reshape(2, 64, 128)

        loop(32, step, 2)

    def fold(i, result):
        spec[:, pl.ds(8 * i, 8), :] = result.reshape(64, 8, 128)

    def unfold(i):
        return spec[:, pl.ds(8 * i, 8), :].reshape(512, 128).astype(BF)

    def branch_third(k):
        def ahead(i):
            lanes = [
                x[8 * i + j, :, pl.ds(16 * k, 16), :].reshape(128, 128) for j in range(8)
            ]
            fold(i, dot_nt(fc[...], jnp.concatenate(lanes, axis=1)))

        loop(8, ahead)
        mix(0)

        def behind(i):
            turned = dot_nt(place[...], unfold(i)).astype(BF)
            result = dot(turned, il[...])
            for j in range(4):
                pair = [
                    result[:, 128 * (2 * j + e) : 128 * (2 * j + e + 1)].reshape(16, 8, 128) for e in range(2)
                ]
                third[pl.ds(16 * k, 16), pl.ds(64 * i + 16 * j, 16), :] = jnp.concatenate(pair, axis=1).astype(BF)

        loop(8, behind)

    def branch_first(k):
        def ahead(i):
            fold(i, dot(fr[...], ra[k, :, pl.ds(64 * i, 64), :].reshape(1024, 128)))

        loop(8, ahead)
        mix(1)

        def behind(i):
            ra[k, :, pl.ds(64 * i, 64), :] = dot(ir[...], unfold(i)).astype(BF).reshape(16, 64, 128)

        loop(8, behind)

    def branch_second(k):
        def ahead(i):
            fold(i, dot(fc[...], rb[k, pl.ds(8 * i, 8)].reshape(1024, 128)))

        loop(8, ahead)
        mix(2)

        def behind(i):
            rb[k, pl.ds(8 * i, 8)] = dot(ic[...], unfold(i)).astype(BF).reshape(8, 4, 32, 128)

        loop(8, behind)

    for i in range(3, 11):
        loads[i].wait()
    branch_third(0)
    branch_third(1)

    def spread(rows, columns):
        a = lax.broadcasted_iota(jnp.int32, (rows, columns), 0)
        b = lax.broadcasted_iota(jnp.int32, (rows, columns), 1)
        return (b // 8 == a).astype(F32).astype(BF)

    def diagonal(columns):
        a = lax.broadcasted_iota(jnp.int32, (8, columns), 0)
        b = lax.broadcasted_iota(jnp.int32, (8, columns), 1)
        return (b % 8 == a).astype(F32)

    widen_in[...] = dot_tn(ffn_in[...], spread(64, 512))
    widen_out[...] = dot(ffn_out[...], spread(256, 2048))

    def widen(src, dst, columns):
        keep = diagonal(columns)

        def step(i):
            pair = [jnp.broadcast_to(src[pl.ds(2 * i + e, 1), :], (8, columns)) * keep for e in range(2)]
            dst[pl.ds(16 * i, 16), :] = jnp.concatenate(pair, axis=0).astype(BF)

        return step

    loop(128, widen(widen_in, wide_in, 512))
    loop(32, widen(widen_out, wide_out, 2048))

    def spread_bias(src, dst, count):
        def step(i):
            rows = lax.broadcasted_iota(jnp.int32, (256, count), 0) + 256 * i
            picked = lax.broadcasted_iota(jnp.int32, (256, count), 1) == rows // 8
            values = jnp.where(picked, jnp.broadcast_to(src[...], (256, count)), 0.0)
            dst[pl.ds(256 * i, 256), :] = jnp.broadcast_to(jnp.sum(values, axis=1, keepdims=True), (256, 128))

        loop(8 * count // 256, step)

    spread_bias(row_in, bias_in, 256)
    spread_bias(row_out, bias_out, 64)

    for i in range(11, 17):
        loads[i].wait()

    def do_first(k):
        own[k].wait()
        for part in parts_of[k]:
            for d in ORDER:
                forward(part, r, lax.rem(r + 16 - d, 16)).wait_recv()
        branch_first(k)
        for d in ORDER:
            give(k, lax.rem(r + d, 16), r).start()
        own_back[k].start()

    def do_second(k):
        own_col[k].wait()
        for d in range(1, 4):
            col_forward(k, q, lax.rem(q + d, 4)).wait_recv()
        branch_second(k)
        for d in range(1, 4):
            col_give(k, lax.rem(q + d, 4), q).start()
        own_col_back[k].start()

    do_first(0)
    do_second(0)
    do_second(1)
    do_first(1)

    for k in range(2):
        own_col_back[k].wait()
        for d in range(1, 4):
            col_give(k, q, lax.rem(q + d, 4)).wait_recv()
        for d in range(1, 4):
            col_forward(k, lax.rem(q + d, 4), q).wait_send()
        for part in parts_of[k]:
            for d in ORDER:
                forward(part, lax.rem(r + d, 16), r).wait_send()

    def add_second(k):
        def step(i):
            for j, part in enumerate(swapped(back2, k, i)):
                at = (pl.ds(16 * k, 16), pl.ds(32 * i + 16 * j, 16), slice(None))
                third[at] = (third[at].astype(F32) + part).astype(BF)

        loop(16, step, 4)

    add_second(0)
    add_second(1)

    def feed(first, second):
        both = (first, second)
        lanes = [(back1[n].astype(F32) + third[n].astype(F32)).astype(BF) for n in both]
        summed = jnp.concatenate(lanes, axis=1)

        def up(i):
            at = pl.ds(512 * i, 512)
            pre = dot(wide_in[at, :], summed)
            bias = bias_in[at, :]
            pre = pre + jnp.concatenate([bias, bias], axis=1)
            hidden[at, :] = (0.5 * pre * (1.0 + lax.erf(pre * ROOT_HALF))).astype(BF)

        loop(4, up, 2)

        result = dot(wide_out[...], hidden[...])
        for j, n in enumerate(both):
            part = result[:, 128 * j : 128 * (j + 1)] + bias_out[...] + xs[n].astype(F32)
            xs[n] = part.astype(BF)

    def out_copy(i):
        at = (pl.ds(4 * i, 4), slice(None), pl.ds(0, 16), slice(None))
        return pltpu.make_async_copy(x.at[at], out_cells.at[pl.ds(4 * i, 4)], out_sem.at[i])

    def row_copy(n):
        return pltpu.make_async_copy(xs.at[16 + n], out_rows.at[n], out_sem.at[16 + n])

    def to_cells(i):
        for j, cells in enumerate(restored(swap_back, [xs[pl.ds(0, 16), pl.ds(32 * i + 16 * j, 16), :] for j in range(2)])):
            x[pl.ds(4 * i + 2 * j, 2), :, pl.ds(0, 16), :] = cells
        out_copy(i).start()

    for k in range(2):
        own_back[k].wait()

        def unit(i):
            sources = [lax.rem(r + 16 - lax.rem(8 - i, 8), 16), lax.rem(r + 8 - i, 16)]

            @pl.when(i > 0)
            def _():
                give(k, r, sources[0]).wait_recv()

            give(k, r, sources[1]).wait_recv()
            feed(16 * k + sources[0], 16 * k + sources[1])
            if k == 1:
                row_copy(sources[0]).start()
                row_copy(sources[1]).start()

        loop(8, unit)
        if k == 0:
            loop(16, to_cells, 4)

    loop(16, lambda i: out_copy(i).wait())
    loop(16, lambda i: row_copy(i).wait())
    for k in range(2):
        for d in range(1, 4):
            col_give(k, lax.rem(q + d, 4), q).wait_send()
        for d in ORDER:
            give(k, lax.rem(r + d, 16), r).wait_send()


def body(ocean_field, spec_first, spec_second, spec_third, ffn_in, ffn_out, bias_in, bias_out):
    consts = constants(128, 32, 8, 16, 16)
    fwd_row, inv_row, fwd_col, inv_col, inv_line, swap, swap_back, place = (jnp.asarray(c) for c in consts)
    anywhere = pl.BlockSpec(memory_space=pl.ANY)
    dma = pltpu.SemaphoreType.DMA
    scratch = [
        pltpu.VMEM((64, 8, 32, 128), BF),
        pltpu.VMEM((32, 512, 128), BF),
        pltpu.VMEM((2, 16, 512, 128), BF),
        pltpu.VMEM((2, 64, 4, 32, 128), BF),
        pltpu.VMEM((32, 512, 128), BF),
        pltpu.VMEM((64, 8, 32, 128), BF),
        pltpu.VMEM((32, 512, 128), BF),
        pltpu.VMEM((64, 64, 128), F32),
        pltpu.VMEM((3, 2, 32, 64, 64), BF),
        pltpu.VMEM((256, 256), BF),
        pltpu.VMEM((256, 256), BF),
        pltpu.VMEM((128, 128), BF),
        pltpu.VMEM((512, 1024), BF),
        pltpu.VMEM((1024, 512), BF),
        pltpu.VMEM((512, 1024), BF),
        pltpu.VMEM((1024, 512), BF),
        pltpu.VMEM((512, 1024), BF),
        pltpu.VMEM((64, 256), BF),
        pltpu.VMEM((64, 256), BF),
        pltpu.VMEM((1, 256), F32),
        pltpu.VMEM((1, 64), F32),
        pltpu.VMEM((2048, 128), F32),
        pltpu.VMEM((512, 128), F32),
        pltpu.VMEM((256, 512), F32),
        pltpu.VMEM((64, 2048), F32),
        pltpu.VMEM((2048, 512), BF),
        pltpu.VMEM((512, 2048), BF),
        pltpu.VMEM((2048, 256), BF),
        dma((17,)), dma((8,)), dma((32,)),
        dma((3, 16)), dma((3, 16)), dma((2, 16)), dma((2, 16)),
        dma((2, 4)), dma((2, 4)), dma((2, 4)), dma((2, 4)),
    ]
    cells, rows = pl.pallas_call(
        kernel,
        out_shape=(jax.ShapeDtypeStruct((64, 8, 16, 128), BF), jax.ShapeDtypeStruct((16, 512, 128), BF)),
        in_specs=[anywhere] * 16,
        out_specs=(anywhere, anywhere),
        scratch_shapes=scratch,
        compiler_params=pltpu.CompilerParams(
            collective_id=0, has_side_effects=True, vmem_limit_bytes=60 * 2**20
        ),
        name="fno_layer",
    )(
        ocean_field, spec_first, spec_second, spec_third, ffn_in, ffn_out.T, bias_in[None, :], bias_out[None, :],
        swap, swap_back, place, fwd_row, inv_row, fwd_col, inv_col, inv_line,
    )
    return pl.pallas_call(
        finish,
        out_shape=jax.ShapeDtypeStruct(ocean_field.shape, BF),
        in_specs=[anywhere] * 3,
        out_specs=anywhere,
        scratch_shapes=[
            pltpu.VMEM((256, 256), BF),
            pltpu.VMEM((16, 512, 128), BF),
            pltpu.VMEM((64, 8, 32, 128), BF),
            dma(()), dma((8,)), dma((8,)), dma((8,)),
        ],
        name="finish",
    )(swap_back, cells, rows)


def solution(mesh):
    return jax.shard_map(
        body,
        mesh=mesh,
        in_specs=(P("grp", "row", "col", None), P(), P(), P(), P(), P(), P(), P()),
        out_specs=P("grp", "row", "col", None),
        check_vma=False,
    )
```

```python
import functools
import math

import jax
import jax.numpy as jnp
import ml_dtypes
import numpy as np
from jax import lax
from jax.experimental import pallas as pl
from jax.experimental.pallas import tpu as pltpu
from jax.sharding import PartitionSpec as P

MESH = pl.DeviceIdType.MESH
BF = jnp.bfloat16
F32 = jnp.float32
ROOT_HALF = math.sqrt(0.5)
ORDER = (8, 7, 9, 6, 10, 5, 11, 4, 12, 3, 13, 2, 14, 1, 15)


def tables(length, modes):
    n = np.arange(length, dtype=np.int32)[:, None]
    m = np.arange(modes, dtype=np.int32)[None, :]
    phase = (n * m % length).astype(np.float32) * np.float32(2.0 * math.pi / length)
    cos, sin = np.cos(phase).astype(np.float32), np.sin(phase).astype(np.float32)
    forward = np.stack([cos, -sin], axis=2).reshape(length, 2 * modes)
    factor = (np.where(m == 0, 1.0, 2.0) / length).astype(np.float32)
    inverse = np.stack([factor * cos, -factor * sin], axis=2).reshape(length, 2 * modes)
    return forward.astype(ml_dtypes.bfloat16), inverse.astype(ml_dtypes.bfloat16)


def constants(length, modes, rows, peers, half):
    forward, inverse = (t.astype(np.float32) for t in tables(length, modes))
    eye = np.eye(8, dtype=np.float32)
    k = 2 * modes
    split = forward.reshape(peers, rows, k)
    fwd_row = np.einsum("pnk,cd->kcpdn", split, eye).reshape(k * 8, length * 8)
    fwd_col = np.einsum("nk,cd->kcdn", forward, eye).reshape(k * 8, length * 8)
    split = inverse.reshape(peers, rows, k)
    inv_row = np.einsum("pnk,cd->pcnkd", split, eye).reshape(length * 8, k * 8)
    inv_col = np.einsum("nk,cd->cnkd", inverse, eye).reshape(length * 8, k * 8)
    inv_line = np.ascontiguousarray(inv_col.T)
    swap = np.zeros((half, 2, rows, 2, rows, half), np.float32)
    place = np.zeros((half, rows, rows, half), np.float32)
    for a in range(half):
        for b in range(rows):
            place[a, b, b, a] = 1.0
            for c in range(2):
                swap[a, c, b, c, b, a] = 1.0
    swap = swap.reshape(2 * half * rows, 2 * half * rows)
    place = place.reshape(half * rows, half * rows)
    return [t.astype(ml_dtypes.bfloat16) for t in (fwd_row, inv_row, fwd_col, inv_col, inv_line, swap, swap.T, place)]


def dot(a, b):
    return jnp.dot(a, b, preferred_element_type=F32)


def dot_nt(a, b):
    return lax.dot_general(a, b, (((1,), (1,)), ((), ())), preferred_element_type=F32)


def dot_tn(a, b):
    return lax.dot_general(a, b, (((0,), (0,)), ((), ())), preferred_element_type=F32)


def loop(count, body, wide=1):
    def step(i, carry):
        for j in range(wide):
            body(i * wide + j)
        return carry

    lax.fori_loop(0, count // wide, step, 0)


def restored(swap_back, blocks):
    both = dot(swap_back[...], jnp.concatenate([b.reshape(256, 128) for b in blocks], axis=1))
    return [both[:, 128 * j : 128 * (j + 1)].astype(BF).reshape(2, 8, 16, 128) for j in range(2)]


def finish(back_hbm, cells, rows, out, swap_back, held, staged, table_sem, cell_sem, load_sem, out_sem):
    table = pltpu.make_async_copy(back_hbm, swap_back, table_sem)

    def load(i):
        at = (slice(None), pl.ds(128 * i, 128))
        return pltpu.make_async_copy(rows.at[at], held.at[at], load_sem.at[i])

    def move(i):
        at = pl.ds(16 * i, 16)
        return pltpu.make_async_copy(cells.at[at], staged.at[at, :, 0:16], cell_sem.at[i])

    def store(i):
        at = pl.ds(16 * i, 16)
        return pltpu.make_async_copy(staged.at[at], out.at[at], out_sem.at[i])

    table.start()
    for i in range(4):
        load(i).start()
        move(i).start()
    table.wait()

    def step(i):
        load(i).wait()
        for e in range(4):
            blocks = [held[:, pl.ds(128 * i + 32 * e + 16 * j, 16), :] for j in range(2)]
            for j, part in enumerate(restored(swap_back, blocks)):
                staged[pl.ds(16 * i + 4 * e + 2 * j, 2), :, 16:32, :] = part
        move(i).wait()
        store(i).start()

    loop(4, step)
    for i in range(4):
        store(i).wait()


def kernel(
    x_hbm, s1_hbm, s2_hbm, s3_hbm, fi_hbm, fo_hbm, bi_hbm, bo_hbm,
    swap_hbm, back_hbm, place_hbm, fr_hbm, ir_hbm, fc_hbm, ic_hbm, il_hbm,
    out_cells, out_rows,
    x, xs, ra, rb, back1, back2, third, spec, mix_w, swap, swap_back, place, fr, ir, fc, ic, il,
    ffn_in, ffn_out, row_in, row_out, bias_in, bias_out,
    widen_in, widen_out, wide_in, wide_out, hidden,
    load_sem, own_sem, out_sem, fwd_s, fwd_r, ret_s, ret_r, cf_s, cf_r, cr_s, cr_r,
):
    g, r, q = lax.axis_index("grp"), lax.axis_index("row"), lax.axis_index("col")
    loads = [
        pltpu.make_async_copy(src, dst, load_sem.at[i])
        for i, (src, dst) in enumerate(
            [
                (x_hbm.at[:32], x.at[:32]), (swap_hbm, swap), (x_hbm.at[32:], x.at[32:]), (s3_hbm, mix_w.at[0]), (fc_hbm, fc), (il_hbm, il), (place_hbm, place),
                (fi_hbm, ffn_in), (fo_hbm, ffn_out), (bi_hbm, row_in), (bo_hbm, row_out), (fr_hbm, fr),
                (ir_hbm, ir), (ic_hbm, ic), (s1_hbm, mix_w.at[1]), (s2_hbm, mix_w.at[2]), (back_hbm, swap_back),
            ]
        )
    ]
    for c in loads:
        c.start()

    barrier = pltpu.get_barrier_semaphore()
    for d in range(1, 16):
        pl.semaphore_signal(barrier, inc=1, device_id=(g, lax.rem(r + d, 16), q), device_id_type=MESH)
    for d in range(1, 4):
        pl.semaphore_signal(barrier, inc=1, device_id=(g, r, lax.rem(q + d, 4)), device_id_type=MESH)

    def forward(part, t, s):
        k, at = ((0, pl.ds(0, 256)), (0, pl.ds(256, 256)), (1, pl.ds(0, 512)))[part]
        return pltpu.make_async_remote_copy(
            xs.at[k * 16 + t, at], ra.at[k, s, at], fwd_s.at[part, t], fwd_r.at[part, s],
            device_id=(g, t, q), device_id_type=MESH,
        )

    parts_of = ((0, 1), (2,))

    def give(k, t, s):
        return pltpu.make_async_remote_copy(
            ra.at[k, t], back1.at[k * 16 + s], ret_s.at[k, t], ret_r.at[k, s], device_id=(g, t, q), device_id_type=MESH
        )

    def col_forward(k, t, s):
        return pltpu.make_async_remote_copy(
            x.at[:, 2 * t + k], rb.at[k, :, s], cf_s.at[k, t], cf_r.at[k, s], device_id=(g, r, t), device_id_type=MESH
        )

    def col_give(k, t, s):
        return pltpu.make_async_remote_copy(
            rb.at[k, :, t], back2.at[:, 2 * s + k], cr_s.at[k, t], cr_r.at[k, s], device_id=(g, r, t), device_id_type=MESH
        )

    own = [pltpu.make_async_copy(xs.at[k * 16 + r], ra.at[k, r], own_sem.at[k]) for k in range(2)]
    own_back = [pltpu.make_async_copy(ra.at[k, r], back1.at[k * 16 + r], own_sem.at[2 + k]) for k in range(2)]
    own_col = [pltpu.make_async_copy(x.at[:, 2 * q + k], rb.at[k, :, q], own_sem.at[4 + k]) for k in range(2)]
    own_col_back = [
        pltpu.make_async_copy(rb.at[k, :, q], back2.at[:, 2 * q + k], own_sem.at[6 + k]) for k in range(2)
    ]

    def swapped(ref, k, i):
        parts = [
            ref[pl.ds(4 * i + 2 * j, 2), :, pl.ds(16 * k, 16), :].reshape(256, 128) for j in range(2)
        ]
        both = dot(swap[...], jnp.concatenate(parts, axis=1))
        return [both[:, 128 * j : 128 * (j + 1)].reshape(16, 16, 128) for j in range(2)]

    def to_rows(k, start, count):
        def step(i):
            for j, part in enumerate(swapped(x, k, start + i)):
                xs[pl.ds(16 * k, 16), pl.ds(32 * (start + i) + 16 * j, 16), :] = part.astype(BF)

        loop(count, step, 4)

    loads[0].wait()
    loads[1].wait()
    to_rows(0, 0, 8)
    pl.semaphore_wait(barrier, 18)
    for d in ORDER:
        forward(0, lax.rem(r + d, 16), r).start()
    loads[2].wait()
    to_rows(0, 8, 8)
    for d in ORDER:
        forward(1, lax.rem(r + d, 16), r).start()
    own[0].start()
    for k in range(2):
        own_col[k].start()
        for d in range(1, 4):
            col_forward(k, lax.rem(q + d, 4), q).start()
    to_rows(1, 0, 16)
    for d in ORDER:
        forward(2, lax.rem(r + d, 16), r).start()
    own[1].start()

    def transposed_mix(d):
        def step(m):
            re = mix_w[d, 0, m].astype(F32)
            im = mix_w[d, 1, m].astype(F32)
            upper = jnp.concatenate([re, im], axis=1)
            lower = jnp.concatenate([-im, re], axis=1)
            return jnp.concatenate([upper, lower], axis=0).T.astype(BF)

        return step

    def mix(d):
        matrix = transposed_mix(d)

        def step(m):
            rhs = spec[pl.ds(2 * m, 2)].reshape(128, 128).astype(BF)
            spec[pl.ds(2 * m, 2)] = dot(matrix(m), rhs).reshape(2, 64, 128)

        loop(32, step, 2)

    def fold(i, result):
        spec[:, pl.ds(8 * i, 8), :] = result.reshape(64, 8, 128)

    def unfold(i):
        return spec[:, pl.ds(8 * i, 8), :].reshape(512, 128).astype(BF)

    def branch_third(k):
        def ahead(i):
            lanes = [
                x[8 * i + j, :, pl.ds(16 * k, 16), :].reshape(128, 128) for j in range(8)
            ]
            fold(i, dot_nt(fc[...], jnp.concatenate(lanes, axis=1)))

        loop(8, ahead)
        mix(0)

        def behind(i):
            turned = dot_nt(place[...], unfold(i)).astype(BF)
            result = dot(turned, il[...])
            for j in range(4):
                pair = [
                    result[:, 128 * (2 * j + e) : 128 * (2 * j + e + 1)].reshape(16, 8, 128) for e in range(2)
                ]
                third[pl.ds(16 * k, 16), pl.ds(64 * i + 16 * j, 16), :] = jnp.concatenate(pair, axis=1).astype(BF)

        loop(8, behind)

    def branch_first(k):
        def ahead(i):
            fold(i, dot(fr[...], ra[k, :, pl.ds(64 * i, 64), :].reshape(1024, 128)))

        loop(8, ahead)
        mix(1)

        def behind(i):
            ra[k, :, pl.ds(64 * i, 64), :] = dot(ir[...], unfold(i)).astype(BF).reshape(16, 64, 128)

        loop(8, behind)

    def branch_second(k):
        def ahead(i):
            fold(i, dot(fc[...], rb[k, pl.ds(8 * i, 8)].reshape(1024, 128)))

        loop(8, ahead)
        mix(2)

        def behind(i):
            rb[k, pl.ds(8 * i, 8)] = dot(ic[...], unfold(i)).astype(BF).reshape(8, 4, 32, 128)

        loop(8, behind)

    for i in range(3, 11):
        loads[i].wait()
    branch_third(0)
    branch_third(1)

    def spread(rows, columns):
        a = lax.broadcasted_iota(jnp.int32, (rows, columns), 0)
        b = lax.broadcasted_iota(jnp.int32, (rows, columns), 1)
        return (b // 8 == a).astype(F32).astype(BF)

    def diagonal(columns):
        a = lax.broadcasted_iota(jnp.int32, (8, columns), 0)
        b = lax.broadcasted_iota(jnp.int32, (8, columns), 1)
        return (b % 8 == a).astype(F32)

    widen_in[...] = dot_tn(ffn_in[...], spread(64, 512))
    widen_out[...] = dot(ffn_out[...], spread(256, 2048))

    def widen(src, dst, columns):
        keep = diagonal(columns)

        def step(i):
            pair = [jnp.broadcast_to(src[pl.ds(2 * i + e, 1), :], (8, columns)) * keep for e in range(2)]
            dst[pl.ds(16 * i, 16), :] = jnp.concatenate(pair, axis=0).astype(BF)

        return step

    loop(128, widen(widen_in, wide_in, 512))
    loop(32, widen(widen_out, wide_out, 2048))

    def spread_bias(src, dst, count):
        def step(i):
            rows = lax.broadcasted_iota(jnp.int32, (256, count), 0) + 256 * i
            picked = lax.broadcasted_iota(jnp.int32, (256, count), 1) == rows // 8
            values = jnp.where(picked, jnp.broadcast_to(src[...], (256, count)), 0.0)
            dst[pl.ds(256 * i, 256), :] = jnp.broadcast_to(jnp.sum(values, axis=1, keepdims=True), (256, 128))

        loop(8 * count // 256, step)

    spread_bias(row_in, bias_in, 256)
    spread_bias(row_out, bias_out, 64)

    for i in range(11, 17):
        loads[i].wait()

    def do_first(k):
        own[k].wait()
        for part in parts_of[k]:
            for d in ORDER:
                forward(part, r, lax.rem(r + 16 - d, 16)).wait_recv()
        branch_first(k)
        for d in ORDER[::-1]:
            give(k, lax.rem(r + d, 16), r).start()
        own_back[k].start()

    def do_second(k):
        own_col[k].wait()
        for d in range(1, 4):
            col_forward(k, q, lax.rem(q + d, 4)).wait_recv()
        branch_second(k)
        for d in range(1, 4):
            col_give(k, lax.rem(q + d, 4), q).start()
        own_col_back[k].start()

    do_first(0)
    do_second(0)
    do_second(1)
    do_first(1)

    for k in range(2):
        own_col_back[k].wait()
        for d in range(1, 4):
            col_give(k, q, lax.rem(q + d, 4)).wait_recv()
        for d in range(1, 4):
            col_forward(k, lax.rem(q + d, 4), q).wait_send()
        for part in parts_of[k]:
            for d in ORDER:
                forward(part, lax.rem(r + d, 16), r).wait_send()

    def add_second(k):
        def step(i):
            for j, part in enumerate(swapped(back2, k, i)):
                at = (pl.ds(16 * k, 16), pl.ds(32 * i + 16 * j, 16), slice(None))
                third[at] = (third[at].astype(F32) + part).astype(BF)

        loop(16, step, 4)

    add_second(0)
    add_second(1)

    def feed(first, second):
        both = (first, second)
        lanes = [(back1[n].astype(F32) + third[n].astype(F32)).astype(BF) for n in both]
        summed = jnp.concatenate(lanes, axis=1)

        def up(i):
            at = pl.ds(512 * i, 512)
            pre = dot(wide_in[at, :], summed)
            bias = bias_in[at, :]
            pre = pre + jnp.concatenate([bias, bias], axis=1)
            hidden[at, :] = (0.5 * pre * (1.0 + lax.erf(pre * ROOT_HALF))).astype(BF)

        loop(4, up, 2)

        result = dot(wide_out[...], hidden[...])
        for j, n in enumerate(both):
            part = result[:, 128 * j : 128 * (j + 1)] + bias_out[...] + xs[n].astype(F32)
            xs[n] = part.astype(BF)

    def out_copy(i):
        at = (pl.ds(4 * i, 4), slice(None), pl.ds(0, 16), slice(None))
        return pltpu.make_async_copy(x.at[at], out_cells.at[pl.ds(4 * i, 4)], out_sem.at[i])

    def row_copy(n):
        return pltpu.make_async_copy(xs.at[16 + n], out_rows.at[n], out_sem.at[16 + n])

    def to_cells(i):
        for j, cells in enumerate(restored(swap_back, [xs[pl.ds(0, 16), pl.ds(32 * i + 16 * j, 16), :] for j in range(2)])):
            x[pl.ds(4 * i + 2 * j, 2), :, pl.ds(0, 16), :] = cells
        out_copy(i).start()

    for k in range(2):
        own_back[k].wait()

        def unit(i):
            sources = [lax.rem(r + 16 - lax.rem(i + 1, 8), 16), lax.rem(r + 1 + i, 16)]

            @pl.when(i < 7)
            def _():
                give(k, r, sources[0]).wait_recv()

            give(k, r, sources[1]).wait_recv()
            feed(16 * k + sources[0], 16 * k + sources[1])
            if k == 1:
                row_copy(sources[0]).start()
                row_copy(sources[1]).start()

        loop(8, unit)
        if k == 0:
            loop(16, to_cells, 4)

    loop(16, lambda i: out_copy(i).wait())
    loop(16, lambda i: row_copy(i).wait())
    for k in range(2):
        for d in range(1, 4):
            col_give(k, lax.rem(q + d, 4), q).wait_send()
        for d in ORDER:
            give(k, lax.rem(r + d, 16), r).wait_send()


def body(ocean_field, spec_first, spec_second, spec_third, ffn_in, ffn_out, bias_in, bias_out):
    consts = constants(128, 32, 8, 16, 16)
    fwd_row, inv_row, fwd_col, inv_col, inv_line, swap, swap_back, place = (jnp.asarray(c) for c in consts)
    anywhere = pl.BlockSpec(memory_space=pl.ANY)
    dma = pltpu.SemaphoreType.DMA
    scratch = [
        pltpu.VMEM((64, 8, 32, 128), BF),
        pltpu.VMEM((32, 512, 128), BF),
        pltpu.VMEM((2, 16, 512, 128), BF),
        pltpu.VMEM((2, 64, 4, 32, 128), BF),
        pltpu.VMEM((32, 512, 128), BF),
        pltpu.VMEM((64, 8, 32, 128), BF),
        pltpu.VMEM((32, 512, 128), BF),
        pltpu.VMEM((64, 64, 128), F32),
        pltpu.VMEM((3, 2, 32, 64, 64), BF),
        pltpu.VMEM((256, 256), BF),
        pltpu.VMEM((256, 256), BF),
        pltpu.VMEM((128, 128), BF),
        pltpu.VMEM((512, 1024), BF),
        pltpu.VMEM((1024, 512), BF),
        pltpu.VMEM((512, 1024), BF),
        pltpu.VMEM((1024, 512), BF),
        pltpu.VMEM((512, 1024), BF),
        pltpu.VMEM((64, 256), BF),
        pltpu.VMEM((64, 256), BF),
        pltpu.VMEM((1, 256), F32),
        pltpu.VMEM((1, 64), F32),
        pltpu.VMEM((2048, 128), F32),
        pltpu.VMEM((512, 128), F32),
        pltpu.VMEM((256, 512), F32),
        pltpu.VMEM((64, 2048), F32),
        pltpu.VMEM((2048, 512), BF),
        pltpu.VMEM((512, 2048), BF),
        pltpu.VMEM((2048, 256), BF),
        dma((17,)), dma((8,)), dma((32,)),
        dma((3, 16)), dma((3, 16)), dma((2, 16)), dma((2, 16)),
        dma((2, 4)), dma((2, 4)), dma((2, 4)), dma((2, 4)),
    ]
    cells, rows = pl.pallas_call(
        kernel,
        out_shape=(jax.ShapeDtypeStruct((64, 8, 16, 128), BF), jax.ShapeDtypeStruct((16, 512, 128), BF)),
        in_specs=[anywhere] * 16,
        out_specs=(anywhere, anywhere),
        scratch_shapes=scratch,
        compiler_params=pltpu.CompilerParams(
            collective_id=0, has_side_effects=True, vmem_limit_bytes=60 * 2**20
        ),
        name="fno_layer",
    )(
        ocean_field, spec_first, spec_second, spec_third, ffn_in, ffn_out.T, bias_in[None, :], bias_out[None, :],
        swap, swap_back, place, fwd_row, inv_row, fwd_col, inv_col, inv_line,
    )
    return pl.pallas_call(
        finish,
        out_shape=jax.ShapeDtypeStruct(ocean_field.shape, BF),
        in_specs=[anywhere] * 3,
        out_specs=anywhere,
        scratch_shapes=[
            pltpu.VMEM((256, 256), BF),
            pltpu.VMEM((16, 512, 128), BF),
            pltpu.VMEM((64, 8, 32, 128), BF),
            dma(()), dma((4,)), dma((4,)), dma((4,)),
        ],
        name="finish",
    )(swap_back, cells, rows)


def solution(mesh):
    return jax.shard_map(
        body,
        mesh=mesh,
        in_specs=(P("grp", "row", "col", None), P(), P(), P(), P(), P(), P(), P()),
        out_specs=P("grp", "row", "col", None),
        check_vma=False,
    )
```

```python
import functools
import math

import jax
import jax.numpy as jnp
import ml_dtypes
import numpy as np
from jax import lax
from jax.experimental import pallas as pl
from jax.experimental.pallas import tpu as pltpu
from jax.sharding import PartitionSpec as P

MESH = pl.DeviceIdType.MESH
BF = jnp.bfloat16
F32 = jnp.float32
ROOT_HALF = math.sqrt(0.5)
ORDER = (8, 7, 9, 6, 10, 5, 11, 4, 12, 3, 13, 2, 14, 1, 15)


def tables(length, modes):
    n = np.arange(length, dtype=np.int32)[:, None]
    m = np.arange(modes, dtype=np.int32)[None, :]
    phase = (n * m % length).astype(np.float32) * np.float32(2.0 * math.pi / length)
    cos, sin = np.cos(phase).astype(np.float32), np.sin(phase).astype(np.float32)
    forward = np.stack([cos, -sin], axis=2).reshape(length, 2 * modes)
    factor = (np.where(m == 0, 1.0, 2.0) / length).astype(np.float32)
    inverse = np.stack([factor * cos, -factor * sin], axis=2).reshape(length, 2 * modes)
    return forward.astype(ml_dtypes.bfloat16), inverse.astype(ml_dtypes.bfloat16)


def constants(length, modes, rows, peers, half):
    forward, inverse = (t.astype(np.float32) for t in tables(length, modes))
    eye = np.eye(8, dtype=np.float32)
    k = 2 * modes
    split = forward.reshape(peers, rows, k)
    fwd_row = np.einsum("pnk,cd->kcpdn", split, eye).reshape(k * 8, length * 8)
    fwd_col = np.einsum("nk,cd->kcdn", forward, eye).reshape(k * 8, length * 8)
    split = inverse.reshape(peers, rows, k)
    inv_row = np.einsum("pnk,cd->pcnkd", split, eye).reshape(length * 8, k * 8)
    inv_col = np.einsum("nk,cd->cnkd", inverse, eye).reshape(length * 8, k * 8)
    inv_line = np.ascontiguousarray(inv_col.T)
    swap = np.zeros((half, 2, rows, 2, rows, half), np.float32)
    place = np.zeros((half, rows, rows, half), np.float32)
    for a in range(half):
        for b in range(rows):
            place[a, b, b, a] = 1.0
            for c in range(2):
                swap[a, c, b, c, b, a] = 1.0
    swap = swap.reshape(2 * half * rows, 2 * half * rows)
    place = place.reshape(half * rows, half * rows)
    return [t.astype(ml_dtypes.bfloat16) for t in (fwd_row, inv_row, fwd_col, inv_col, inv_line, swap, swap.T, place)]


def dot(a, b):
    return jnp.dot(a, b, preferred_element_type=F32)


def dot_nt(a, b):
    return lax.dot_general(a, b, (((1,), (1,)), ((), ())), preferred_element_type=F32)


def dot_tn(a, b):
    return lax.dot_general(a, b, (((0,), (0,)), ((), ())), preferred_element_type=F32)


def loop(count, body, wide=1):
    def step(i, carry):
        for j in range(wide):
            body(i * wide + j)
        return carry

    lax.fori_loop(0, count // wide, step, 0)


def restored(swap_back, blocks):
    both = dot(swap_back[...], jnp.concatenate([b.reshape(256, 128) for b in blocks], axis=1))
    return [both[:, 128 * j : 128 * (j + 1)].astype(BF).reshape(2, 8, 16, 128) for j in range(2)]


def finish(back_hbm, cells, rows, out, swap_back, held, staged, table_sem, cell_sem, load_sem, out_sem):
    table = pltpu.make_async_copy(back_hbm, swap_back, table_sem)

    def load(i):
        at = (slice(None), pl.ds(128 * i, 128))
        return pltpu.make_async_copy(rows.at[at], held.at[at], load_sem.at[i])

    def move(i):
        at = pl.ds(16 * i, 16)
        return pltpu.make_async_copy(cells.at[at], staged.at[at, :, 0:16], cell_sem.at[i])

    def store(i):
        at = pl.ds(16 * i, 16)
        return pltpu.make_async_copy(staged.at[at], out.at[at], out_sem.at[i])

    table.start()
    for i in range(4):
        load(i).start()
        move(i).start()
    table.wait()

    def step(i):
        load(i).wait()
        for e in range(4):
            blocks = [held[:, pl.ds(128 * i + 32 * e + 16 * j, 16), :] for j in range(2)]
            for j, part in enumerate(restored(swap_back, blocks)):
                staged[pl.ds(16 * i + 4 * e + 2 * j, 2), :, 16:32, :] = part
        move(i).wait()
        store(i).start()

    loop(4, step)
    for i in range(4):
        store(i).wait()


def kernel(
    x_hbm, s1_hbm, s2_hbm, s3_hbm, fi_hbm, fo_hbm, bi_hbm, bo_hbm,
    swap_hbm, back_hbm, place_hbm, fr_hbm, ir_hbm, fc_hbm, ic_hbm, il_hbm,
    out_cells, out_rows,
    x, xs, ra, rb, back1, back2, third, spec, mix_w, swap, swap_back, place, fr, ir, fc, ic, il,
    ffn_in, ffn_out, row_in, row_out, bias_in, bias_out,
    widen_in, widen_out, wide_in, wide_out, hidden,
    load_sem, own_sem, out_sem, fwd_s, fwd_r, ret_s, ret_r, cf_s, cf_r, cr_s, cr_r,
):
    g, r, q = lax.axis_index("grp"), lax.axis_index("row"), lax.axis_index("col")
    loads = [
        pltpu.make_async_copy(src, dst, load_sem.at[i])
        for i, (src, dst) in enumerate(
            [
                (x_hbm.at[:16], x.at[:16]), (swap_hbm, swap), (x_hbm.at[16:], x.at[16:]), (s3_hbm, mix_w.at[0]), (fc_hbm, fc), (il_hbm, il), (place_hbm, place),
                (fi_hbm, ffn_in), (fo_hbm, ffn_out), (bi_hbm, row_in), (bo_hbm, row_out), (fr_hbm, fr),
                (ir_hbm, ir), (ic_hbm, ic), (s1_hbm, mix_w.at[1]), (s2_hbm, mix_w.at[2]), (back_hbm, swap_back),
            ]
        )
    ]
    for c in loads:
        c.start()

    barrier = pltpu.get_barrier_semaphore()
    for d in range(1, 16):
        pl.semaphore_signal(barrier, inc=1, device_id=(g, lax.rem(r + d, 16), q), device_id_type=MESH)
    for d in range(1, 4):
        pl.semaphore_signal(barrier, inc=1, device_id=(g, r, lax.rem(q + d, 4)), device_id_type=MESH)

    def forward(part, t, s):
        k, at = ((0, pl.ds(0, 128)), (0, pl.ds(128, 384)), (1, pl.ds(0, 512)))[part]
        return pltpu.make_async_remote_copy(
            xs.at[k * 16 + t, at], ra.at[k, s, at], fwd_s.at[part, t], fwd_r.at[part, s],
            device_id=(g, t, q), device_id_type=MESH,
        )

    parts_of = ((0, 1), (2,))

    def give(k, t, s):
        return pltpu.make_async_remote_copy(
            ra.at[k, t], back1.at[k * 16 + s], ret_s.at[k, t], ret_r.at[k, s], device_id=(g, t, q), device_id_type=MESH
        )

    def col_forward(k, t, s):
        return pltpu.make_async_remote_copy(
            x.at[:, 2 * t + k], rb.at[k, :, s], cf_s.at[k, t], cf_r.at[k, s], device_id=(g, r, t), device_id_type=MESH
        )

    def col_give(k, t, s):
        return pltpu.make_async_remote_copy(
            rb.at[k, :, t], back2.at[:, 2 * s + k], cr_s.at[k, t], cr_r.at[k, s], device_id=(g, r, t), device_id_type=MESH
        )

    own = [pltpu.make_async_copy(xs.at[k * 16 + r], ra.at[k, r], own_sem.at[k]) for k in range(2)]
    own_back = [pltpu.make_async_copy(ra.at[k, r], back1.at[k * 16 + r], own_sem.at[2 + k]) for k in range(2)]
    own_col = [pltpu.make_async_copy(x.at[:, 2 * q + k], rb.at[k, :, q], own_sem.at[4 + k]) for k in range(2)]
    own_col_back = [
        pltpu.make_async_copy(rb.at[k, :, q], back2.at[:, 2 * q + k], own_sem.at[6 + k]) for k in range(2)
    ]

    def swapped(ref, k, i):
        parts = [
            ref[pl.ds(4 * i + 2 * j, 2), :, pl.ds(16 * k, 16), :].reshape(256, 128) for j in range(2)
        ]
        both = dot(swap[...], jnp.concatenate(parts, axis=1))
        return [both[:, 128 * j : 128 * (j + 1)].reshape(16, 16, 128) for j in range(2)]

    def to_rows(k, start, count):
        def step(i):
            for j, part in enumerate(swapped(x, k, start + i)):
                xs[pl.ds(16 * k, 16), pl.ds(32 * (start + i) + 16 * j, 16), :] = part.astype(BF)

        loop(count, step, 4)

    loads[0].wait()
    loads[1].wait()
    to_rows(0, 0, 4)
    pl.semaphore_wait(barrier, 18)
    for d in ORDER:
        forward(0, lax.rem(r + d, 16), r).start()
    loads[2].wait()
    to_rows(0, 4, 12)
    for d in ORDER:
        forward(1, lax.rem(r + d, 16), r).start()
    own[0].start()
    for k in range(2):
        own_col[k].start()
        for d in range(1, 4):
            col_forward(k, lax.rem(q + d, 4), q).start()
    to_rows(1, 0, 16)
    for d in ORDER:
        forward(2, lax.rem(r + d, 16), r).start()
    own[1].start()

    def transposed_mix(d):
        def step(m):
            re = mix_w[d, 0, m].astype(F32)
            im = mix_w[d, 1, m].astype(F32)
            upper = jnp.concatenate([re, im], axis=1)
            lower = jnp.concatenate([-im, re], axis=1)
            return jnp.concatenate([upper, lower], axis=0).T.astype(BF)

        return step

    def mix(d):
        matrix = transposed_mix(d)

        def step(m):
            rhs = spec[pl.ds(2 * m, 2)].reshape(128, 128).astype(BF)
            spec[pl.ds(2 * m, 2)] = dot(matrix(m), rhs).reshape(2, 64, 128)

        loop(32, step, 2)

    def fold(i, result):
        spec[:, pl.ds(8 * i, 8), :] = result.reshape(64, 8, 128)

    def unfold(i):
        return spec[:, pl.ds(8 * i, 8), :].reshape(512, 128).astype(BF)

    def branch_third(k):
        def ahead(i):
            lanes = [
                x[8 * i + j, :, pl.ds(16 * k, 16), :].reshape(128, 128) for j in range(8)
            ]
            fold(i, dot_nt(fc[...], jnp.concatenate(lanes, axis=1)))

        loop(8, ahead)
        mix(0)

        def behind(i):
            turned = dot_nt(place[...], unfold(i)).astype(BF)
            result = dot(turned, il[...])
            for j in range(4):
                pair = [
                    result[:, 128 * (2 * j + e) : 128 * (2 * j + e + 1)].reshape(16, 8, 128) for e in range(2)
                ]
                third[pl.ds(16 * k, 16), pl.ds(64 * i + 16 * j, 16), :] = jnp.concatenate(pair, axis=1).astype(BF)

        loop(8, behind)

    def branch_first(k):
        def ahead(i):
            fold(i, dot(fr[...], ra[k, :, pl.ds(64 * i, 64), :].reshape(1024, 128)))

        loop(8, ahead)
        mix(1)

        def behind(i):
            ra[k, :, pl.ds(64 * i, 64), :] = dot(ir[...], unfold(i)).astype(BF).reshape(16, 64, 128)

        loop(8, behind)

    def branch_second(k):
        def ahead(i):
            fold(i, dot(fc[...], rb[k, pl.ds(8 * i, 8)].reshape(1024, 128)))

        loop(8, ahead)
        mix(2)

        def behind(i):
            rb[k, pl.ds(8 * i, 8)] = dot(ic[...], unfold(i)).astype(BF).reshape(8, 4, 32, 128)

        loop(8, behind)

    for i in range(3, 11):
        loads[i].wait()
    branch_third(0)
    branch_third(1)

    def spread(rows, columns):
        a = lax.broadcasted_iota(jnp.int32, (rows, columns), 0)
        b = lax.broadcasted_iota(jnp.int32, (rows, columns), 1)
        return (b // 8 == a).astype(F32).astype(BF)

    def diagonal(columns):
        a = lax.broadcasted_iota(jnp.int32, (8, columns), 0)
        b = lax.broadcasted_iota(jnp.int32, (8, columns), 1)
        return (b % 8 == a).astype(F32)

    widen_in[...] = dot_tn(ffn_in[...], spread(64, 512))
    widen_out[...] = dot(ffn_out[...], spread(256, 2048))

    def widen(src, dst, columns):
        keep = diagonal(columns)

        def step(i):
            pair = [jnp.broadcast_to(src[pl.ds(2 * i + e, 1), :], (8, columns)) * keep for e in range(2)]
            dst[pl.ds(16 * i, 16), :] = jnp.concatenate(pair, axis=0).astype(BF)

        return step

    loop(128, widen(widen_in, wide_in, 512))
    loop(32, widen(widen_out, wide_out, 2048))

    def spread_bias(src, dst, count):
        def step(i):
            rows = lax.broadcasted_iota(jnp.int32, (256, count), 0) + 256 * i
            picked = lax.broadcasted_iota(jnp.int32, (256, count), 1) == rows // 8
            values = jnp.where(picked, jnp.broadcast_to(src[...], (256, count)), 0.0)
            dst[pl.ds(256 * i, 256), :] = jnp.broadcast_to(jnp.sum(values, axis=1, keepdims=True), (256, 128))

        loop(8 * count // 256, step)

    spread_bias(row_in, bias_in, 256)
    spread_bias(row_out, bias_out, 64)

    for i in range(11, 17):
        loads[i].wait()

    def do_first(k):
        own[k].wait()
        for part in parts_of[k]:
            for d in ORDER:
                forward(part, r, lax.rem(r + 16 - d, 16)).wait_recv()
        branch_first(k)
        for d in ORDER[::-1]:
            give(k, lax.rem(r + d, 16), r).start()
        own_back[k].start()

    def do_second(k):
        own_col[k].wait()
        for d in range(1, 4):
            col_forward(k, q, lax.rem(q + d, 4)).wait_recv()
        branch_second(k)
        for d in range(1, 4):
            col_give(k, lax.rem(q + d, 4), q).start()
        own_col_back[k].start()

    do_first(0)
    do_second(0)
    do_second(1)
    do_first(1)

    for k in range(2):
        own_col_back[k].wait()
        for d in range(1, 4):
            col_give(k, q, lax.rem(q + d, 4)).wait_recv()
        for d in range(1, 4):
            col_forward(k, lax.rem(q + d, 4), q).wait_send()
        for part in parts_of[k]:
            for d in ORDER:
                forward(part, lax.rem(r + d, 16), r).wait_send()

    def add_second(k):
        def step(i):
            for j, part in enumerate(swapped(back2, k, i)):
                at = (pl.ds(16 * k, 16), pl.ds(32 * i + 16 * j, 16), slice(None))
                third[at] = (third[at].astype(F32) + part).astype(BF)

        loop(16, step, 4)

    add_second(0)
    add_second(1)

    def feed(first, second):
        both = (first, second)
        lanes = [(back1[n].astype(F32) + third[n].astype(F32)).astype(BF) for n in both]
        summed = jnp.concatenate(lanes, axis=1)

        def up(i):
            at = pl.ds(512 * i, 512)
            pre = dot(wide_in[at, :], summed)
            bias = bias_in[at, :]
            pre = pre + jnp.concatenate([bias, bias], axis=1)
            hidden[at, :] = (0.5 * pre * (1.0 + lax.erf(pre * ROOT_HALF))).astype(BF)

        loop(4, up, 2)

        result = dot(wide_out[...], hidden[...])
        for j, n in enumerate(both):
            part = result[:, 128 * j : 128 * (j + 1)] + bias_out[...] + xs[n].astype(F32)
            xs[n] = part.astype(BF)

    def out_copy(i):
        at = (pl.ds(4 * i, 4), slice(None), pl.ds(0, 16), slice(None))
        return pltpu.make_async_copy(x.at[at], out_cells.at[pl.ds(4 * i, 4)], out_sem.at[i])

    def row_copy(n):
        return pltpu.make_async_copy(xs.at[16 + n], out_rows.at[n], out_sem.at[16 + n])

    def to_cells(i):
        for j, cells in enumerate(restored(swap_back, [xs[pl.ds(0, 16), pl.ds(32 * i + 16 * j, 16), :] for j in range(2)])):
            x[pl.ds(4 * i + 2 * j, 2), :, pl.ds(0, 16), :] = cells
        out_copy(i).start()

    for k in range(2):
        own_back[k].wait()

        def unit(i):
            sources = [lax.rem(r + 16 - lax.rem(i + 1, 8), 16), lax.rem(r + 1 + i, 16)]

            @pl.when(i < 7)
            def _():
                give(k, r, sources[0]).wait_recv()

            give(k, r, sources[1]).wait_recv()
            feed(16 * k + sources[0], 16 * k + sources[1])
            if k == 1:
                row_copy(sources[0]).start()
                row_copy(sources[1]).start()

        loop(8, unit)
        if k == 0:
            loop(16, to_cells, 4)

    loop(16, lambda i: out_copy(i).wait())
    loop(16, lambda i: row_copy(i).wait())
    for k in range(2):
        for d in range(1, 4):
            col_give(k, lax.rem(q + d, 4), q).wait_send()
        for d in ORDER:
            give(k, lax.rem(r + d, 16), r).wait_send()


def body(ocean_field, spec_first, spec_second, spec_third, ffn_in, ffn_out, bias_in, bias_out):
    consts = constants(128, 32, 8, 16, 16)
    fwd_row, inv_row, fwd_col, inv_col, inv_line, swap, swap_back, place = (jnp.asarray(c) for c in consts)
    anywhere = pl.BlockSpec(memory_space=pl.ANY)
    dma = pltpu.SemaphoreType.DMA
    scratch = [
        pltpu.VMEM((64, 8, 32, 128), BF),
        pltpu.VMEM((32, 512, 128), BF),
        pltpu.VMEM((2, 16, 512, 128), BF),
        pltpu.VMEM((2, 64, 4, 32, 128), BF),
        pltpu.VMEM((32, 512, 128), BF),
        pltpu.VMEM((64, 8, 32, 128), BF),
        pltpu.VMEM((32, 512, 128), BF),
        pltpu.VMEM((64, 64, 128), F32),
        pltpu.VMEM((3, 2, 32, 64, 64), BF),
        pltpu.VMEM((256, 256), BF),
        pltpu.VMEM((256, 256), BF),
        pltpu.VMEM((128, 128), BF),
        pltpu.VMEM((512, 1024), BF),
        pltpu.VMEM((1024, 512), BF),
        pltpu.VMEM((512, 1024), BF),
        pltpu.VMEM((1024, 512), BF),
        pltpu.VMEM((512, 1024), BF),
        pltpu.VMEM((64, 256), BF),
        pltpu.VMEM((64, 256), BF),
        pltpu.VMEM((1, 256), F32),
        pltpu.VMEM((1, 64), F32),
        pltpu.VMEM((2048, 128), F32),
        pltpu.VMEM((512, 128), F32),
        pltpu.VMEM((256, 512), F32),
        pltpu.VMEM((64, 2048), F32),
        pltpu.VMEM((2048, 512), BF),
        pltpu.VMEM((512, 2048), BF),
        pltpu.VMEM((2048, 256), BF),
        dma((17,)), dma((8,)), dma((32,)),
        dma((3, 16)), dma((3, 16)), dma((2, 16)), dma((2, 16)),
        dma((2, 4)), dma((2, 4)), dma((2, 4)), dma((2, 4)),
    ]
    cells, rows = pl.pallas_call(
        kernel,
        out_shape=(jax.ShapeDtypeStruct((64, 8, 16, 128), BF), jax.ShapeDtypeStruct((16, 512, 128), BF)),
        in_specs=[anywhere] * 16,
        out_specs=(anywhere, anywhere),
        scratch_shapes=scratch,
        compiler_params=pltpu.CompilerParams(
            collective_id=0, has_side_effects=True, vmem_limit_bytes=60 * 2**20
        ),
        name="fno_layer",
    )(
        ocean_field, spec_first, spec_second, spec_third, ffn_in, ffn_out.T, bias_in[None, :], bias_out[None, :],
        swap, swap_back, place, fwd_row, inv_row, fwd_col, inv_col, inv_line,
    )
    return pl.pallas_call(
        finish,
        out_shape=jax.ShapeDtypeStruct(ocean_field.shape, BF),
        in_specs=[anywhere] * 3,
        out_specs=anywhere,
        scratch_shapes=[
            pltpu.VMEM((256, 256), BF),
            pltpu.VMEM((16, 512, 128), BF),
            pltpu.VMEM((64, 8, 32, 128), BF),
            dma(()), dma((4,)), dma((4,)), dma((4,)),
        ],
        name="finish",
    )(swap_back, cells, rows)


def solution(mesh):
    return jax.shard_map(
        body,
        mesh=mesh,
        in_specs=(P("grp", "row", "col", None), P(), P(), P(), P(), P(), P(), P()),
        out_specs=P("grp", "row", "col", None),
        check_vma=False,
    )
```
